128 devices in a mesh: seq: 32 (over y, z, core), chan: 4 (over x).
Axes of the slice: x: 4, y: 4, z: 4, core: 2. Of those that a mesh axis runs over, the one named last changes fastest.
Arguments:
- streams: bfloat16 [3, 256, 32768], P(None, 'chan', 'seq'), may hold values from -6 to 6
- short_taps: float32 [3, 256, 3], P(None, 'chan'), may hold values from -3 to 3
- long_filter: float32 [256, 32768], P('chan', 'seq'), may hold values from -0.03125 to 0.03125
- skip_gain: float32 [256], P('chan'), may hold values from -4 to 4
Outputs:
- gated: bfloat16 [256, 32768], P('chan', 'seq')
The draws below stay inside these ranges and needn't reach their ends.
All inputs are finite; a program needn't handle non-finite values.
Results may differ from the reference program's by a relative error of at most 0.001.
Values may be sent and summed in bfloat16 or wider, within the bound.
A program may use at most 64 MiB of HBM per device.

```python
import jax
import jax.numpy as jnp
from jax import lax

CHANNELS = 256
LENGTH = 32768


def levels(own_key, extent, pieces, smallest, high):
    factor_of = 1.0
    for axis_at, shards_of in pieces:
        draws = jax.random.uniform(jax.random.fold_in(jax.random.fold_in(own_key, 6), axis_at), (shards_of,), jnp.float32, smallest / len(pieces), high / len(pieces))
        factor_of = factor_of * jnp.repeat(jnp.exp(draws), extent[axis_at] // shards_of).reshape((-1,) + (1,) * (len(extent) - 1 - axis_at))
    return factor_of


def scatter_about(key, dims, scale, bound, shards=(), kind=jnp.bfloat16):
    gain = levels(key, dims, shards, -0.22, 0.18) if shards else 1.0
    values = jax.random.normal(key, dims, jnp.float32) * scale * gain
    return jnp.minimum(jnp.maximum(values, -bound), bound).astype(kind)


def setup_inputs(seed: int = 0) -> dict:
    arg_keys = jax.random.split(jax.random.key(seed), 5)
    return {
        "streams": scatter_about(arg_keys[0], (3, CHANNELS, LENGTH), 1.0, 6.0, ((1, 4), (2, 32))),
        "short_taps": scatter_about(arg_keys[1], (3, CHANNELS, 3), 0.6, 3.0, ((1, 4),), jnp.float32),
        "long_filter": scatter_about(arg_keys[2], (CHANNELS, LENGTH), LENGTH ** -0.5, 0.03125, ((0, 4), (1, 32)), jnp.float32),
        "skip_gain": scatter_about(arg_keys[3], (CHANNELS,), 1.0, 4.0, ((0, 4),), jnp.float32),
    }


def one_channel(pair):
    signal, kernel = pair
    points = 2 * LENGTH
    spectrum = jnp.fft.rfft(signal, n=points) * jnp.fft.rfft(kernel, n=points)
    return jnp.fft.irfft(spectrum, n=points)[:LENGTH].astype(signal.dtype)


def reference(streams, short_taps, long_filter, skip_gain):
    widened = jnp.pad(streams.astype(jnp.float32), ((0, 0), (0, 0), (2, 0)))
    short = short_taps[:, :, 0:1] * widened[:, :, 2:]
    short = short + short_taps[:, :, 1:2] * widened[:, :, 1:-1]
    short = short + short_taps[:, :, 2:3] * widened[:, :, :-2]
    mixed = short[1] * short[2]
    conv = lax.map(one_channel, (mixed, long_filter))
    return (short[0] * (conv + skip_gain[:, None] * mixed)).astype(jnp.bfloat16)
```

```python
import functools
import math

import jax
import jax.numpy as jnp
import ml_dtypes
import numpy as np
from jax import lax
from jax.experimental import pallas as pl
from jax.experimental.pallas import tpu as pltpu
from jax.sharding import PartitionSpec as P

LANES = 128
OWN = 2


def halves(table):
    high = table.astype(ml_dtypes.bfloat16)
    low = (table - high.astype(np.float64)).astype(ml_dtypes.bfloat16)
    return np.stack([high, low])


def tables(rows):
    row = np.arange(rows)
    lane = np.arange(LANES)
    angle = (2.0 * math.pi / (4 * rows)) * ((2 * row[:, None] + 1) * row[None, :] % (4 * rows))
    outer = np.concatenate([np.cos(angle), -np.sin(angle)], axis=0)
    outer_back = outer.T / (rows * LANES)
    angle = (2.0 * math.pi / LANES) * (lane[:, None] * lane[None, :] % LANES)
    cos, sin = np.cos(angle), np.sin(angle)
    inner = np.block([[cos, -sin], [sin, cos]])
    angle = (2.0 * math.pi / (4 * rows * LANES)) * ((2 * row[:, None] + 1) * lane[None, :])
    turn = np.stack([np.cos(angle), np.sin(angle)]).astype(np.float32)
    return halves(outer), halves(outer_back), np.concatenate([halves(inner), halves(inner.T)]), turn


def split(x):
    high = x.astype(jnp.bfloat16)
    return high, (x - high.astype(jnp.float32)).astype(jnp.bfloat16)


def dot(a, b):
    return jnp.dot(a, b, preferred_element_type=jnp.float32)


def left(table, x):
    high, low = split(x)
    return dot(table[0], high) + dot(table[0], low) + dot(table[1], high)


def right(x, high_table, low_table):
    high, low = split(x)
    return dot(high, high_table) + dot(low, high_table) + dot(high, low_table)


def forward(x, rows, outer, inner, turn):
    part = left(outer, x)
    cos, sin = turn[0], turn[1]
    turned = []
    for c in range(OWN):
        re = part[:rows, c * LANES:(c + 1) * LANES]
        im = part[rows:, c * LANES:(c + 1) * LANES]
        turned.append(jnp.concatenate([re * cos + im * sin, im * cos - re * sin], axis=1))
    return right(jnp.concatenate(turned, axis=0), inner[0], inner[1])


def backward(y, rows, outer_back, inner, turn):
    part = right(y, inner[2], inner[3])
    cos, sin = turn[0], turn[1]
    re_parts, im_parts = [], []
    for c in range(OWN):
        re = part[c * rows:(c + 1) * rows, :LANES]
        im = part[c * rows:(c + 1) * rows, LANES:]
        re_parts.append(re * cos - im * sin)
        im_parts.append(im * cos + re * sin)
    turned = jnp.concatenate(
        [jnp.concatenate(re_parts, axis=1), jnp.concatenate(im_parts, axis=1)], axis=0
    )
    return left(outer_back, turned)


def multiply(a, b):
    a_re, a_im, b_re, b_im = a[:, :LANES], a[:, LANES:], b[:, :LANES], b[:, LANES:]
    return jnp.concatenate([a_re * b_re - a_im * b_im, a_re * b_im + a_im * b_re], axis=1)


def short_conv(x, taps, lane, first):
    one = pltpu.roll(x, 1, 1)
    two = pltpu.roll(x, 2, 1)
    one_up = jnp.where(first, 0.0, pltpu.roll(one, 1, 0))
    two_up = jnp.where(first, 0.0, pltpu.roll(two, 1, 0))
    one = jnp.where(lane < 1, one_up, one)
    two = jnp.where(lane < 2, two_up, two)
    return taps[0] * x + taps[1] * one + taps[2] * two


def kernel(
    peers, streams_hbm, filter_hbm, taps_ref, skip_ref, outer_hbm, back_hbm, inner_hbm, turn_hbm,
    out_ref,
    streams, filt, outer, back, inner, turn,
    filter_out, filter_in, wide, pair_out, pair_in, query_out, query_in, gated_out, gated_in,
    load_sem, send_sem, recv_sem,
):
    rows = 8 * peers
    channels = OWN * peers
    me = lax.axis_index("seq")
    barrier = pltpu.get_barrier_semaphore()

    def load(i, source, target):
        copy = pltpu.make_async_copy(source, target, load_sem.at[i])
        copy.start()
        return copy

    filter_load = load(0, filter_hbm, filt)
    streams_load = load(1, streams_hbm, streams)
    table_loads = [
        load(2, outer_hbm, outer), load(3, turn_hbm, turn), load(4, inner_hbm, inner), load(5, back_hbm, back)
    ]

    def each_peer(step):
        def turn_to(d, carry):
            step(lax.rem(me + d, peers))
            return carry

        lax.fori_loop(1, peers, turn_to, 0)

    def greet(peer):
        pl.semaphore_signal(
            barrier, inc=1, device_id={"seq": peer}, device_id_type=pl.DeviceIdType.MESH
        )

    each_peer(greet)

    def send(source, target, index):
        def to(peer):
            pltpu.make_async_remote_copy(
                src_ref=source.at[peer],
                dst_ref=target.at[me],
                send_sem=send_sem.at[index],
                recv_sem=recv_sem.at[index],
                device_id={"seq": peer},
                device_id_type=pl.DeviceIdType.MESH,
            ).start()

        each_peer(to)
        target[me] = source[me]

    def wait(buffer, sem):
        others = buffer.at[pl.ds(0, peers - 1)]
        pltpu.make_async_copy(others, others, sem).wait()

    def regroup(values, target):
        for t in range(8):
            wide[pl.ds(t, channels, stride=8), :] = values(t)
        target(wide[...].reshape(peers, OWN * 8, LANES))

    filter_load.wait()

    def put_filter(v):
        filter_out[...] = v

    regroup(lambda t: filt[:, t * LANES:(t + 1) * LANES], put_filter)
    pl.semaphore_wait(barrier, peers - 1)
    send(filter_out, filter_in, 0)

    streams_load.wait()

    def stream(s):
        return lambda t: streams[s, :, t * LANES:(t + 1) * LANES].astype(jnp.float32)

    def put_pair(s):
        def put(v):
            pair_out[:, s * 16:(s + 1) * 16, :] = v.astype(jnp.bfloat16)

        return put

    regroup(stream(1), put_pair(0))
    regroup(stream(2), put_pair(1))
    send(pair_out, pair_in, 1)

    def put_query(v):
        query_out[...] = v.astype(jnp.bfloat16)

    regroup(stream(0), put_query)
    send(query_out, query_in, 2)

    for copy in table_loads:
        copy.wait()
    wait(filter_in, recv_sem.at[0])

    def by_channel(v):
        parts = [v[:, 8 * c:8 * c + 8, :].reshape(rows, LANES) for c in range(OWN)]
        return jnp.concatenate(parts, axis=1)

    filter_bins = forward(by_channel(filter_in[...]), rows, outer, inner, turn)

    lane = lax.broadcasted_iota(jnp.int32, (rows, LANES), 1)
    first = lax.broadcasted_iota(jnp.int32, (rows, LANES), 0) < 1

    def shorted(v, s, c):
        own = OWN * me + c
        taps = [taps_ref[(s * channels + own) * 3 + i] for i in range(3)]
        return short_conv(v[:, 8 * c:8 * c + 8, :].reshape(rows, LANES), taps, lane, first)

    wait(pair_in, recv_sem.at[1])
    key = pair_in[:, 0:16, :].astype(jnp.float32)
    value = pair_in[:, 16:32, :].astype(jnp.float32)
    mixed = jnp.concatenate(
        [shorted(key, 1, c) * shorted(value, 2, c) for c in range(OWN)], axis=1
    )
    bins = forward(mixed, rows, outer, inner, turn)
    conv = backward(multiply(bins, filter_bins), rows, back, inner, turn)

    wait(query_in, recv_sem.at[2])
    query = query_in[...].astype(jnp.float32)
    results = []
    for c in range(OWN):
        cut = slice(c * LANES, (c + 1) * LANES)
        gated = shorted(query, 0, c) * (conv[:, cut] + skip_ref[OWN * me + c] * mixed[:, cut])
        results.append(gated.reshape(peers, 8, LANES))
    gated_out[...] = jnp.concatenate(results, axis=1).astype(jnp.bfloat16)
    send(gated_out, gated_in, 3)

    wait(filter_out, send_sem.at[0])
    wait(pair_out, send_sem.at[1])
    wait(query_out, send_sem.at[2])
    wait(gated_in, recv_sem.at[3])
    wide[...] = gated_in[...].astype(jnp.float32).reshape(peers * OWN * 8, LANES)
    for t in range(8):
        out_ref[:, t * LANES:(t + 1) * LANES] = wide[pl.ds(t, channels, stride=8), :].astype(jnp.bfloat16)
    wait(gated_out, send_sem.at[3])


def body(streams, short_taps, long_filter, skip_gain):
    peers = lax.axis_size("seq")
    rows = 8 * peers
    outer, back, inner, turn = (jnp.asarray(t) for t in tables(rows))
    anywhere = pl.BlockSpec(memory_space=pl.ANY)
    scalars = pl.BlockSpec(memory_space=pltpu.SMEM)
    f32, bf16 = jnp.float32, jnp.bfloat16
    one = (peers, OWN * 8, LANES)
    two = (peers, 2 * OWN * 8, LANES)
    vmem = pltpu.VMEM
    return pl.pallas_call(
        functools.partial(kernel, peers),
        out_shape=jax.ShapeDtypeStruct(long_filter.shape, bf16),
        in_specs=[anywhere, anywhere, scalars, scalars] + [anywhere] * 4,
        out_specs=pl.BlockSpec(memory_space=pltpu.VMEM),
        scratch_shapes=[
            vmem(streams.shape, bf16), vmem(long_filter.shape, f32),
            vmem(outer.shape, bf16), vmem(back.shape, bf16), vmem(inner.shape, bf16), vmem(turn.shape, f32),
            vmem(one, f32), vmem(one, f32), vmem((peers * OWN * 8, LANES), f32),
            vmem(two, bf16), vmem(two, bf16), vmem(one, bf16), vmem(one, bf16), vmem(one, bf16), vmem(one, bf16),
            pltpu.SemaphoreType.DMA((6,)), pltpu.SemaphoreType.DMA((4,)), pltpu.SemaphoreType.DMA((4,)),
        ],
        compiler_params=pltpu.CompilerParams(
            collective_id=0, has_side_effects=True, vmem_limit_bytes=48 * 1024 * 1024
        ),
    )(streams, long_filter, short_taps.reshape(-1), skip_gain, outer, back, inner, turn)


def solution(mesh):
    return jax.shard_map(
        body,
        mesh=mesh,
        in_specs=(P(None, "chan", "seq"), P(None, "chan", None), P("chan", "seq"), P("chan")),
        out_specs=P("chan", "seq"),
        check_vma=False,
    )
```

```python
import functools
import math

import jax
import jax.numpy as jnp
import ml_dtypes
import numpy as np
from jax import lax
from jax.experimental import pallas as pl
from jax.experimental.pallas import tpu as pltpu
from jax.sharding import PartitionSpec as P

LANES = 128
OWN = 2
VMEM_LIMIT = 60 * 1024 * 1024


def halves(table):
    high = table.astype(ml_dtypes.bfloat16)
    low = (table - high.astype(np.float64)).astype(ml_dtypes.bfloat16)
    return np.stack([high, low])


def tables(rows):
    row = np.arange(rows)
    lane = np.arange(LANES)
    angle = (2.0 * math.pi / (4 * rows)) * ((2 * row[:, None] + 1) * row[None, :] % (4 * rows))
    outer = np.concatenate([np.cos(angle), -np.sin(angle)], axis=0)
    outer_back = outer.T / (rows * LANES)
    angle = (2.0 * math.pi / LANES) * (lane[:, None] * lane[None, :] % LANES)
    cos, sin = np.cos(angle), np.sin(angle)
    inner = np.block([[cos, -sin], [sin, cos]])
    angle = (2.0 * math.pi / (4 * rows * LANES)) * ((2 * row[:, None] + 1) * lane[None, :])
    turn = np.stack([np.cos(angle), np.sin(angle)]).astype(np.float32)
    return halves(outer), halves(outer_back), np.concatenate([halves(inner), halves(inner.T)]), turn


def split(x):
    high = x.astype(jnp.bfloat16)
    return high, (x - high.astype(jnp.float32)).astype(jnp.bfloat16)


def dot(a, b):
    return jnp.dot(a, b, preferred_element_type=jnp.float32)


def left(table, x):
    high, low = split(x)
    return dot(table[0], high) + dot(table[0], low) + dot(table[1], high)


def right(x, high_table, low_table):
    high, low = split(x)
    return dot(high, high_table) + dot(low, high_table) + dot(high, low_table)


def forward(x, rows, outer, inner, turn):
    part = left(outer, x)
    cos, sin = turn[0], turn[1]
    turned = []
    for c in range(OWN):
        re = part[:rows, c * LANES:(c + 1) * LANES]
        im = part[rows:, c * LANES:(c + 1) * LANES]
        turned.append(jnp.concatenate([re * cos + im * sin, im * cos - re * sin], axis=1))
    return right(jnp.concatenate(turned, axis=0), inner[0], inner[1])


def backward(y, rows, outer_back, inner, turn):
    part = right(y, inner[2], inner[3])
    cos, sin = turn[0], turn[1]
    re_parts, im_parts = [], []
    for c in range(OWN):
        re = part[c * rows:(c + 1) * rows, :LANES]
        im = part[c * rows:(c + 1) * rows, LANES:]
        re_parts.append(re * cos - im * sin)
        im_parts.append(im * cos + re * sin)
    turned = jnp.concatenate(
        [jnp.concatenate(re_parts, axis=1), jnp.concatenate(im_parts, axis=1)], axis=0
    )
    return left(outer_back, turned)


def multiply(a, b):
    a_re, a_im, b_re, b_im = a[:, :LANES], a[:, LANES:], b[:, :LANES], b[:, LANES:]
    return jnp.concatenate([a_re * b_re - a_im * b_im, a_re * b_im + a_im * b_re], axis=1)


def short_conv(x, taps, lane, first):
    one = pltpu.roll(x, 1, 1)
    two = pltpu.roll(x, 2, 1)
    one_up = jnp.where(first, 0.0, pltpu.roll(one, 1, 0))
    two_up = jnp.where(first, 0.0, pltpu.roll(two, 1, 0))
    one = jnp.where(lane < 1, one_up, one)
    two = jnp.where(lane < 2, two_up, two)
    return taps[0] * x + taps[1] * one + taps[2] * two


def kernel(
    peers, streams_hbm, filter_hbm, taps_hbm, skip_hbm, outer_hbm, back_hbm, inner_hbm, turn_hbm,
    out_ref,
    streams, filt, taps_v, skip_v, outer, back, inner, turn,
    filter_out, filter_in, wide, pair_out, pair_in, query_out, query_in, gated_out, gated_in,
    load_sem, send_sem, recv_sem,
):
    rows = 8 * peers
    channels = OWN * peers
    me = lax.axis_index("seq")
    barrier = pltpu.get_barrier_semaphore()

    def load(i, source, target):
        copy = pltpu.make_async_copy(source, target, load_sem.at[i])
        copy.start()
        return copy

    filter_load = load(0, filter_hbm, filt)
    streams_load = load(1, streams_hbm, streams)
    table_loads = [
        load(2, outer_hbm, outer), load(3, turn_hbm, turn), load(4, inner_hbm, inner), load(5, back_hbm, back),
        load(6, taps_hbm, taps_v), load(7, skip_hbm, skip_v),
    ]

    def each_peer(step):
        def turn_to(d, carry):
            step(lax.rem(me + d, peers))
            return carry

        lax.fori_loop(1, peers, turn_to, 0)

    def greet(peer):
        pl.semaphore_signal(
            barrier, inc=1, device_id={"seq": peer}, device_id_type=pl.DeviceIdType.MESH
        )

    each_peer(greet)

    def send(source, target, index):
        def to(peer):
            pltpu.make_async_remote_copy(
                src_ref=source.at[peer],
                dst_ref=target.at[me],
                send_sem=send_sem.at[index],
                recv_sem=recv_sem.at[index],
                device_id={"seq": peer},
                device_id_type=pl.DeviceIdType.MESH,
            ).start()

        each_peer(to)
        target[me] = source[me]

    def wait(buffer, sem):
        others = buffer.at[pl.ds(0, peers - 1)]
        pltpu.make_async_copy(others, others, sem).wait()

    def regroup(values, target):
        for t in range(8):
            wide[pl.ds(t, channels, stride=8), :] = values(t)
        target(wide[...].reshape(peers, OWN * 8, LANES))

    filter_load.wait()

    def put_filter(v):
        filter_out[...] = v

    regroup(lambda t: filt[:, t * LANES:(t + 1) * LANES], put_filter)
    pl.semaphore_wait(barrier, peers - 1)
    send(filter_out, filter_in, 0)

    streams_load.wait()

    def stream(s):
        return lambda t: streams[s, :, t * LANES:(t + 1) * LANES].astype(jnp.float32)

    def put_pair(s):
        def put(v):
            pair_out[:, s * 16:(s + 1) * 16, :] = v.astype(jnp.bfloat16)

        return put

    regroup(stream(1), put_pair(0))
    regroup(stream(2), put_pair(1))
    send(pair_out, pair_in, 1)

    def put_query(v):
        query_out[...] = v.astype(jnp.bfloat16)

    regroup(stream(0), put_query)
    send(query_out, query_in, 2)

    for copy in table_loads:
        copy.wait()
    wait(filter_in, recv_sem.at[0])

    def by_channel(v):
        parts = [v[:, 8 * c:8 * c + 8, :].reshape(rows, LANES) for c in range(OWN)]
        return jnp.concatenate(parts, axis=1)

    filter_bins = forward(by_channel(filter_in[...]), rows, outer, inner, turn)

    lane = lax.broadcasted_iota(jnp.int32, (rows, LANES), 1)
    first = lax.broadcasted_iota(jnp.int32, (rows, LANES), 0) < 1

    channel = lax.broadcasted_iota(jnp.int32, (1, channels), 1)

    def pick(v, own):
        return jnp.sum(jnp.where(channel == own, v, 0.0), axis=1, keepdims=True)

    def shorted(v, s, c):
        own = OWN * me + c
        taps = [pick(taps_v[s, i:i + 1, :], own) for i in range(3)]
        return short_conv(v[:, 8 * c:8 * c + 8, :].reshape(rows, LANES), taps, lane, first)

    wait(pair_in, recv_sem.at[1])
    key = pair_in[:, 0:16, :].astype(jnp.float32)
    value = pair_in[:, 16:32, :].astype(jnp.float32)
    mixed = jnp.concatenate(
        [shorted(key, 1, c) * shorted(value, 2, c) for c in range(OWN)], axis=1
    )
    bins = forward(mixed, rows, outer, inner, turn)
    conv = backward(multiply(bins, filter_bins), rows, back, inner, turn)

    wait(query_in, recv_sem.at[2])
    query = query_in[...].astype(jnp.float32)
    results = []
    for c in range(OWN):
        cut = slice(c * LANES, (c + 1) * LANES)
        gated = shorted(query, 0, c) * (conv[:, cut] + pick(skip_v[...], OWN * me + c) * mixed[:, cut])
        results.append(gated.reshape(peers, 8, LANES))
    gated_out[...] = jnp.concatenate(results, axis=1).astype(jnp.bfloat16)
    send(gated_out, gated_in, 3)

    wait(filter_out, send_sem.at[0])
    wait(pair_out, send_sem.at[1])
    wait(query_out, send_sem.at[2])
    wait(gated_in, recv_sem.at[3])
    wide[...] = gated_in[...].astype(jnp.float32).reshape(peers * OWN * 8, LANES)
    for t in range(8):
        out_ref[:, t * LANES:(t + 1) * LANES] = wide[pl.ds(t, channels, stride=8), :].astype(jnp.bfloat16)
    wait(gated_out, send_sem.at[3])


def body(streams, short_taps, long_filter, skip_gain):
    peers = lax.axis_size("seq")
    rows = 8 * peers
    outer, back, inner, turn = (jnp.asarray(t) for t in tables(rows))
    anywhere = pl.BlockSpec(memory_space=pl.ANY)
    f32, bf16 = jnp.float32, jnp.bfloat16
    one = (peers, OWN * 8, LANES)
    two = (peers, 2 * OWN * 8, LANES)
    vmem = pltpu.VMEM
    taps = jnp.transpose(short_taps, (0, 2, 1))
    skip = skip_gain.reshape(1, -1)
    return pl.pallas_call(
        functools.partial(kernel, peers),
        out_shape=jax.ShapeDtypeStruct(long_filter.shape, bf16),
        in_specs=[anywhere] * 8,
        out_specs=pl.BlockSpec(memory_space=pltpu.VMEM),
        scratch_shapes=[
            vmem(streams.shape, bf16), vmem(long_filter.shape, f32),
            vmem(taps.shape, f32), vmem(skip.shape, f32),
            vmem(outer.shape, bf16), vmem(back.shape, bf16), vmem(inner.shape, bf16), vmem(turn.shape, f32),
            vmem(one, f32), vmem(one, f32), vmem((peers * OWN * 8, LANES), f32),
            vmem(two, bf16), vmem(two, bf16), vmem(one, bf16), vmem(one, bf16), vmem(one, bf16), vmem(one, bf16),
            pltpu.SemaphoreType.DMA((8,)), pltpu.SemaphoreType.DMA((4,)), pltpu.SemaphoreType.DMA((4,)),
        ],
        compiler_params=pltpu.CompilerParams(
            collective_id=0, has_side_effects=True, vmem_limit_bytes=VMEM_LIMIT
        ),
    )(streams, long_filter, taps, skip, outer, back, inner, turn)


def solution(mesh):
    return jax.shard_map(
        body,
        mesh=mesh,
        in_specs=(P(None, "chan", "seq"), P(None, "chan", None), P("chan", "seq"), P("chan")),
        out_specs=P("chan", "seq"),
        check_vma=False,
    )
```

```python
import functools
import math

import jax
import jax.numpy as jnp
import ml_dtypes
import numpy as np
from jax import lax
from jax.experimental import pallas as pl
from jax.experimental.pallas import tpu as pltpu
from jax.sharding import PartitionSpec as P

LANES = 128
OWN = 2
VMEM_LIMIT = 48 * 1024 * 1024


def halves(table):
    high = table.astype(ml_dtypes.bfloat16)
    low = (table - high.astype(np.float64)).astype(ml_dtypes.bfloat16)
    return np.stack([high, low])


def tables(rows):
    row = np.arange(rows)
    lane = np.arange(LANES)
    angle = (2.0 * math.pi / (4 * rows)) * ((2 * row[:, None] + 1) * row[None, :] % (4 * rows))
    outer = np.concatenate([np.cos(angle), -np.sin(angle)], axis=0)
    outer_back = outer.T / (rows * LANES)
    angle = (2.0 * math.pi / LANES) * (lane[:, None] * lane[None, :] % LANES)
    cos, sin = np.cos(angle), np.sin(angle)
    inner = np.block([[cos, -sin], [sin, cos]])
    angle = (2.0 * math.pi / (4 * rows * LANES)) * ((2 * row[:, None] + 1) * lane[None, :])
    turn = np.stack([np.cos(angle), np.sin(angle)]).astype(np.float32)
    return halves(outer), halves(outer_back), np.concatenate([halves(inner), halves(inner.T)]), turn


def far_first(peers):
    steps = [(y, z, core) for y in range(max(1, peers // 8)) for z in range(min(4, peers // 2)) for core in range(2)]
    hops = lambda step: min(step[0], 4 - step[0]) + min(step[1], 4 - step[1])
    return sorted(steps[1:], key=hops, reverse=True)


def split(x):
    high = x.astype(jnp.bfloat16)
    return high, (x - high.astype(jnp.float32)).astype(jnp.bfloat16)


def dot(a, b):
    return jnp.dot(a, b, preferred_element_type=jnp.float32)


def left(table, x):
    high, low = split(x)
    return dot(table[0], high) + dot(table[0], low) + dot(table[1], high)


def right(x, high_table, low_table):
    high, low = split(x)
    return dot(high, high_table) + dot(low, high_table) + dot(high, low_table)


def forward(x, rows, outer, inner, turn):
    part = left(outer, x)
    cos, sin = turn[0], turn[1]
    turned = []
    for c in range(OWN):
        re = part[:rows, c * LANES:(c + 1) * LANES]
        im = part[rows:, c * LANES:(c + 1) * LANES]
        turned.append(jnp.concatenate([re * cos + im * sin, im * cos - re * sin], axis=1))
    return right(jnp.concatenate(turned, axis=0), inner[0], inner[1])


def backward(y, rows, outer_back, inner, turn):
    part = right(y, inner[2], inner[3])
    cos, sin = turn[0], turn[1]
    re_parts, im_parts = [], []
    for c in range(OWN):
        re = part[c * rows:(c + 1) * rows, :LANES]
        im = part[c * rows:(c + 1) * rows, LANES:]
        re_parts.append(re * cos - im * sin)
        im_parts.append(im * cos + re * sin)
    turned = jnp.concatenate(
        [jnp.concatenate(re_parts, axis=1), jnp.concatenate(im_parts, axis=1)], axis=0
    )
    return left(outer_back, turned)


def multiply(a, b):
    a_re, a_im, b_re, b_im = a[:, :LANES], a[:, LANES:], b[:, :LANES], b[:, LANES:]
    return jnp.concatenate([a_re * b_re - a_im * b_im, a_re * b_im + a_im * b_re], axis=1)


def short_conv(x, taps, lane, first):
    one = pltpu.roll(x, 1, 1)
    two = pltpu.roll(x, 2, 1)
    one_up = jnp.where(first, 0.0, pltpu.roll(one, 1, 0))
    two_up = jnp.where(first, 0.0, pltpu.roll(two, 1, 0))
    one = jnp.where(lane < 1, one_up, one)
    two = jnp.where(lane < 2, two_up, two)
    return taps[0] * x + taps[1] * one + taps[2] * two


def kernel(
    peers, streams_hbm, filter_hbm, taps_hbm, skip_hbm, outer_hbm, back_hbm, inner_hbm, turn_hbm,
    out_ref,
    streams, filt, taps_v, skip_v, outer, back, inner, turn,
    filter_out, filter_in, wide, pair_out, pair_in, query_out, query_in, gated_out, gated_in,
    load_sem, send_sem, recv_sem,
):
    rows = 8 * peers
    channels = OWN * peers
    me = lax.axis_index("seq")
    barrier = pltpu.get_barrier_semaphore()

    def load(i, source, target):
        copy = pltpu.make_async_copy(source, target, load_sem.at[i])
        copy.start()
        return copy

    filter_load = load(0, filter_hbm, filt)
    streams_load = load(1, streams_hbm, streams)
    table_loads = [
        load(2, outer_hbm, outer), load(3, turn_hbm, turn), load(4, inner_hbm, inner), load(5, back_hbm, back),
        load(6, taps_hbm, taps_v), load(7, skip_hbm, skip_v),
    ]

    ring_at = [lax.rem(me // 8 + d, 4) * 8 for d in range(4)]
    column_at = [lax.rem(me // 2 % 4 + d, 4) * 2 for d in range(4)]
    core_at = [lax.rem(me % 2 + d, 2) for d in range(2)]

    def each_peer(step):
        for y, z, core in far_first(peers):
            step(ring_at[y] + column_at[z] + core_at[core])

    def greet(peer):
        pl.semaphore_signal(
            barrier, inc=1, device_id={"seq": peer}, device_id_type=pl.DeviceIdType.MESH
        )

    each_peer(greet)

    def send(source, target, index):
        def to(peer):
            pltpu.make_async_remote_copy(
                src_ref=source.at[peer],
                dst_ref=target.at[me],
                send_sem=send_sem.at[index],
                recv_sem=recv_sem.at[index],
                device_id={"seq": peer},
                device_id_type=pl.DeviceIdType.MESH,
            ).start()

        each_peer(to)
        target[me] = source[me]

    def wait(buffer, sem):
        others = buffer.at[pl.ds(0, peers - 1)]
        pltpu.make_async_copy(others, others, sem).wait()

    def regroup(values, target):
        for t in range(8):
            wide[pl.ds(t, channels, stride=8), :] = values(t)
        target(wide[...].reshape(peers, OWN * 8, LANES))

    filter_load.wait()

    def put_filter(v):
        filter_out[...] = v

    regroup(lambda t: filt[:, t * LANES:(t + 1) * LANES], put_filter)
    pl.semaphore_wait(barrier, peers - 1)
    send(filter_out, filter_in, 0)

    streams_load.wait()

    def stream(s):
        return lambda t: streams[s, :, t * LANES:(t + 1) * LANES].astype(jnp.float32)

    def put_pair(s):
        def put(v):
            pair_out[:, s * 16:(s + 1) * 16, :] = v.astype(jnp.bfloat16)

        return put

    regroup(stream(1), put_pair(0))
    regroup(stream(2), put_pair(1))
    send(pair_out, pair_in, 1)

    def put_query(v):
        query_out[...] = v.astype(jnp.bfloat16)

    regroup(stream(0), put_query)
    send(query_out, query_in, 2)

    for copy in table_loads:
        copy.wait()
    wait(filter_in, recv_sem.at[0])

    def by_channel(v):
        parts = [v[:, 8 * c:8 * c + 8, :].reshape(rows, LANES) for c in range(OWN)]
        return jnp.concatenate(parts, axis=1)

    filter_bins = forward(by_channel(filter_in[...]), rows, outer, inner, turn)

    lane = lax.broadcasted_iota(jnp.int32, (rows, LANES), 1)
    first = lax.broadcasted_iota(jnp.int32, (rows, LANES), 0) < 1

    channel = lax.broadcasted_iota(jnp.int32, (1, channels), 1)

    def pick(v, own):
        return jnp.sum(jnp.where(channel == own, v, 0.0), axis=1, keepdims=True)

    def shorted(v, s, c):
        own = OWN * me + c
        taps = [pick(taps_v[s, i:i + 1, :], own) for i in range(3)]
        return short_conv(v[:, 8 * c:8 * c + 8, :].reshape(rows, LANES), taps, lane, first)

    wait(pair_in, recv_sem.at[1])
    key = pair_in[:, 0:16, :].astype(jnp.float32)
    value = pair_in[:, 16:32, :].astype(jnp.float32)
    mixed = jnp.concatenate(
        [shorted(key, 1, c) * shorted(value, 2, c) for c in range(OWN)], axis=1
    )
    bins = forward(mixed, rows, outer, inner, turn)
    conv = backward(multiply(bins, filter_bins), rows, back, inner, turn)

    wait(query_in, recv_sem.at[2])
    query = query_in[...].astype(jnp.float32)
    results = []
    for c in range(OWN):
        cut = slice(c * LANES, (c + 1) * LANES)
        gated = shorted(query, 0, c) * (conv[:, cut] + pick(skip_v[...], OWN * me + c) * mixed[:, cut])
        results.append(gated.reshape(peers, 8, LANES))
    gated_out[...] = jnp.concatenate(results, axis=1).astype(jnp.bfloat16)
    send(gated_out, gated_in, 3)

    wait(filter_out, send_sem.at[0])
    wait(pair_out, send_sem.at[1])
    wait(query_out, send_sem.at[2])
    wait(gated_in, recv_sem.at[3])
    wide[...] = gated_in[...].astype(jnp.float32).reshape(peers * OWN * 8, LANES)
    for t in range(8):
        out_ref[:, t * LANES:(t + 1) * LANES] = wide[pl.ds(t, channels, stride=8), :].astype(jnp.bfloat16)
    wait(gated_out, send_sem.at[3])


def body(streams, short_taps, long_filter, skip_gain):
    peers = lax.axis_size("seq")
    rows = 8 * peers
    outer, back, inner, turn = (jnp.asarray(t) for t in tables(rows))
    anywhere = pl.BlockSpec(memory_space=pl.ANY)
    f32, bf16 = jnp.float32, jnp.bfloat16
    one = (peers, OWN * 8, LANES)
    two = (peers, 2 * OWN * 8, LANES)
    vmem = pltpu.VMEM
    taps = jnp.transpose(short_taps, (0, 2, 1))
    skip = skip_gain.reshape(1, -1)
    operands = (streams, long_filter, taps, skip, outer, back, inner, turn)
    return pl.pallas_call(
        functools.partial(kernel, peers),
        out_shape=vmem(long_filter.shape, bf16),
        in_specs=[anywhere] * 8,
        out_specs=pl.BlockSpec(memory_space=pltpu.VMEM),
        scratch_shapes=[
            vmem(streams.shape, bf16), vmem(long_filter.shape, f32),
            vmem(taps.shape, f32), vmem(skip.shape, f32),
            vmem(outer.shape, bf16), vmem(back.shape, bf16), vmem(inner.shape, bf16), vmem(turn.shape, f32),
            vmem(one, f32), vmem(one, f32), vmem((peers * OWN * 8, LANES), f32),
            vmem(two, bf16), vmem(two, bf16), vmem(one, bf16), vmem(one, bf16), vmem(one, bf16), vmem(one, bf16),
            pltpu.SemaphoreType.DMA((8,)), pltpu.SemaphoreType.DMA((4,)), pltpu.SemaphoreType.DMA((4,)),
        ],
        compiler_params=pltpu.CompilerParams(
            collective_id=0, has_side_effects=True, vmem_limit_bytes=VMEM_LIMIT
        ),
    )(*(pltpu.with_memory_space_constraint(x, pltpu.HBM) for x in operands))


def solution(mesh):
    return jax.shard_map(
        body,
        mesh=mesh,
        in_specs=(P(None, "chan", "seq"), P(None, "chan", None), P("chan", "seq"), P("chan")),
        out_specs=P("chan", "seq"),
        check_vma=False,
    )
```

```python
import functools
import math

import jax
import jax.numpy as jnp
import ml_dtypes
import numpy as np
from jax import lax
from jax.experimental import pallas as pl
from jax.experimental.pallas import tpu as pltpu
from jax.sharding import PartitionSpec as P

LANES = 128
OWN = 2
VMEM_LIMIT = 48 * 1024 * 1024


def halves(table):
    high = table.astype(ml_dtypes.bfloat16)
    low = (table - high.astype(np.float64)).astype(ml_dtypes.bfloat16)
    return np.stack([high, low])


def tables(rows):
    row = np.arange(rows)
    lane = np.arange(LANES)
    angle = (2.0 * math.pi / (4 * rows)) * ((2 * row[:, None] + 1) * row[None, :] % (4 * rows))
    outer = np.concatenate([np.cos(angle), -np.sin(angle)], axis=0)
    outer_back = outer.T / (rows * LANES)
    angle = (2.0 * math.pi / LANES) * (lane[:, None] * lane[None, :] % LANES)
    cos, sin = np.cos(angle), np.sin(angle)
    inner = np.block([[cos, -sin], [sin, cos]])
    angle = (2.0 * math.pi / (4 * rows * LANES)) * ((2 * row[:, None] + 1) * lane[None, :])
    turn = np.stack([np.cos(angle), np.sin(angle)]).astype(np.float32)
    return halves(outer), halves(outer_back), np.concatenate([halves(inner), halves(inner.T)]), turn


def far_first(peers):
    steps = [(y, z, core) for y in range(max(1, peers // 8)) for z in range(min(4, peers // 2)) for core in range(2)]
    hops = lambda step: min(step[0], 4 - step[0]) + min(step[1], 4 - step[1])
    return sorted(steps[1:], key=hops, reverse=True)


def split(x):
    high = x.astype(jnp.bfloat16)
    return high, (x - high.astype(jnp.float32)).astype(jnp.bfloat16)


def dot(a, b):
    return jnp.dot(a, b, preferred_element_type=jnp.float32)


def left(table, x):
    high, low = split(x)
    return dot(table[0], high) + dot(table[0], low) + dot(table[1], high)


def right(x, high_table, low_table):
    high, low = split(x)
    return dot(high, high_table) + dot(low, high_table) + dot(high, low_table)


def forward(x, rows, outer, inner, turn):
    part = left(outer, x)
    cos, sin = turn[0], turn[1]
    turned = []
    for c in range(OWN):
        re = part[:rows, c * LANES:(c + 1) * LANES]
        im = part[rows:, c * LANES:(c + 1) * LANES]
        turned.append(jnp.concatenate([re * cos + im * sin, im * cos - re * sin], axis=1))
    return right(jnp.concatenate(turned, axis=0), inner[0], inner[1])


def backward(y, rows, outer_back, inner, turn, turned):
    part = right(y, inner[2], inner[3])
    cos, sin = turn[0], turn[1]
    for c in range(OWN):
        lanes = slice(c * LANES, (c + 1) * LANES)
        re = part[c * rows:(c + 1) * rows, :LANES]
        im = part[c * rows:(c + 1) * rows, LANES:]
        turned[0, :rows, lanes], turned[1, :rows, lanes] = split(re * cos - im * sin)
        turned[0, rows:, lanes], turned[1, rows:, lanes] = split(im * cos + re * sin)
    high, low = turned[0], turned[1]
    return dot(outer_back[0], high) + dot(outer_back[0], low) + dot(outer_back[1], high)


def multiply(a, b):
    a_re, a_im, b_re, b_im = a[:, :LANES], a[:, LANES:], b[:, :LANES], b[:, LANES:]
    return jnp.concatenate([a_re * b_re - a_im * b_im, a_re * b_im + a_im * b_re], axis=1)


def short_conv(x, taps, lane, first):
    one = pltpu.roll(x, 1, 1)
    two = pltpu.roll(x, 2, 1)
    one_up = jnp.where(first, 0.0, pltpu.roll(one, 1, 0))
    two_up = jnp.where(first, 0.0, pltpu.roll(two, 1, 0))
    one = jnp.where(lane < 1, one_up, one)
    two = jnp.where(lane < 2, two_up, two)
    return taps[0] * x + taps[1] * one + taps[2] * two


def kernel(
    peers, streams_hbm, filter_hbm, taps_hbm, skip_hbm, outer_hbm, back_hbm, inner_hbm, turn_hbm,
    out,
    taps_v, skip_v, outer, back, inner, turn,
    filter_in, pair_in, query_in, wide, gated_out, turned, filt, streams,
    load_sem, own_sem, send_sem, recv_sem,
):
    rows = 8 * peers
    channels = OWN * peers
    me = lax.axis_index("seq")
    ring_at = [lax.rem(me // 8 + d, 4) * 8 for d in range(4)]
    column_at = [lax.rem(me // 2 % 4 + d, 4) * 2 for d in range(4)]
    core_at = [lax.rem(me % 2 + d, 2) for d in range(2)]
    order = [ring_at[y] + column_at[z] + core_at[core] for y, z, core in far_first(peers)]

    barrier = pltpu.get_barrier_semaphore()
    for peer in order:
        pl.semaphore_signal(
            barrier, inc=1, device_id={"seq": peer}, device_id_type=pl.DeviceIdType.MESH
        )

    def load(i, source, target):
        copy = pltpu.make_async_copy(source, target, load_sem.at[i])
        copy.start()
        return copy

    own_loads = [load(6, streams_hbm, streams), load(7, filter_hbm, filt)]
    loads = [
        load(0, outer_hbm, outer), load(1, turn_hbm, turn), load(2, inner_hbm, inner),
        load(3, back_hbm, back), load(4, taps_hbm, taps_v), load(5, skip_hbm, skip_v),
    ]

    links = (
        (lambda p: filt.at[p // 4, :, p % 4], lambda p: filter_in.at[p]),
        (lambda p: streams.at[pl.ds(1, 2), p // 4, :, p % 4], lambda p: pair_in.at[:, p]),
        (lambda p: streams.at[0, p // 4, :, p % 4], lambda p: query_in.at[p]),
        (lambda p: gated_out.at[p], lambda p: out.at[p // 4, :, p % 4]),
    )

    def start(index, peer):
        source_of, target_of = links[index]
        pltpu.make_async_remote_copy(
            src_ref=source_of(peer),
            dst_ref=target_of(me),
            send_sem=send_sem.at[index],
            recv_sem=recv_sem.at[index],
            device_id={"seq": peer},
            device_id_type=pl.DeviceIdType.MESH,
        ).start()

    def keep(index):
        source_of, target_of = links[index]
        own = pltpu.make_async_copy(source_of(me), target_of(me), own_sem.at[index])
        own.start()
        return own

    def wait(others, sem):
        pltpu.make_async_copy(others, others, sem).wait()

    for copy in own_loads:
        copy.wait()
    owns = [keep(index) for index in range(3)]
    pl.semaphore_wait(barrier, peers - 1)
    for index in (1, 0, 2):
        for peer in order:
            start(index, peer)
    rest = pl.ds(0, peers - 1)
    for copy in loads:
        copy.wait()

    def one_channel(ref, c):
        return ref[pl.ds(c, rows, stride=OWN), :]

    lane = lax.broadcasted_iota(jnp.int32, (rows, LANES), 1)
    first = lax.broadcasted_iota(jnp.int32, (rows, LANES), 0) < 1
    channel = lax.broadcasted_iota(jnp.int32, (1, channels), 1)

    def pick(v, own):
        return jnp.sum(jnp.where(channel == own, v, 0.0), axis=1, keepdims=True)

    def shorted(ref, s):
        wide[s] = ref.reshape(OWN * rows, LANES)[...].astype(jnp.float32)
        results = []
        for c in range(OWN):
            taps = [pick(taps_v[s, i:i + 1, :], OWN * me + c) for i in range(3)]
            results.append(short_conv(one_channel(wide.at[s], c), taps, lane, first))
        return results

    owns[1].wait()
    wait(pair_in.at[:, rest], recv_sem.at[1])
    key, value = shorted(pair_in.at[0], 1), shorted(pair_in.at[1], 2)
    mixed = [k * v for k, v in zip(key, value)]
    bins = forward(jnp.concatenate(mixed, axis=1), rows, outer, inner, turn)
    owns[0].wait()
    wait(filter_in.at[rest], recv_sem.at[0])
    pairs = filter_in.reshape(OWN * rows, LANES)
    taken = jnp.concatenate([one_channel(pairs, c) for c in range(OWN)], axis=1)
    filter_bins = forward(taken, rows, outer, inner, turn)

    conv = backward(multiply(bins, filter_bins), rows, back, inner, turn, turned)

    owns[2].wait()
    wait(query_in.at[rest], recv_sem.at[2])
    query = shorted(query_in, 0)
    for c in range(OWN):
        gain = pick(skip_v[...], OWN * me + c)
        gated = query[c] * (conv[:, c * LANES:(c + 1) * LANES] + gain * mixed[c])
        wide[3, pl.ds(c, rows, stride=OWN), :] = gated
    gated_out.reshape(OWN * rows, LANES)[...] = wide[3].astype(jnp.bfloat16)
    for peer in range(2):
        pl.when(me != peer)(functools.partial(start, 3, peer))
    for peer in order:
        pl.when(peer >= 2)(functools.partial(start, 3, peer))
    own = keep(3)

    wait(filter_in.at[rest], send_sem.at[0])
    wait(pair_in.at[:, rest], send_sem.at[1])
    wait(query_in.at[rest], send_sem.at[2])
    wait(gated_out.at[rest], send_sem.at[3])
    own.wait()
    wait(gated_out.at[rest], recv_sem.at[3])


def in_pairs(x):
    lead, channels = x.shape[:-2], x.shape[-2]
    x = x.reshape(lead + (channels // 8, 8, 8, LANES))
    return jnp.swapaxes(x, -3, -2).reshape(lead + (channels // 8, 8, 4, OWN, LANES))


def out_of_pairs(x):
    groups = x.shape[0]
    x = jnp.swapaxes(x.reshape(groups, 8, 8, LANES), 1, 2)
    return x.reshape(groups * 8, 8 * LANES)


def body(streams, short_taps, long_filter, skip_gain):
    peers = lax.axis_size("seq")
    rows = 8 * peers
    outer, back, inner, turn = (jnp.asarray(t) for t in tables(rows))
    f32, bf16 = jnp.float32, jnp.bfloat16
    vmem = pltpu.VMEM
    taps = jnp.transpose(short_taps, (0, 2, 1))
    skip = skip_gain.reshape(1, -1)
    operands = (in_pairs(streams), in_pairs(long_filter), taps, skip, outer, back, inner, turn)
    anywhere = pl.BlockSpec(memory_space=pl.ANY)
    one = (peers, 8, OWN, LANES)
    result = pl.pallas_call(
        functools.partial(kernel, peers),
        out_shape=vmem((OWN * peers // 8, 8, 4, OWN, LANES), bf16),
        in_specs=[anywhere] * len(operands),
        out_specs=anywhere,
        scratch_shapes=[
            vmem(taps.shape, f32), vmem(skip.shape, f32),
            vmem(outer.shape, bf16), vmem(back.shape, bf16), vmem(inner.shape, bf16), vmem(turn.shape, f32),
            vmem(one, f32), vmem((2,) + one, bf16), vmem(one, bf16),
            vmem((4, OWN * rows, LANES), f32), vmem(one, bf16), vmem((2, 2 * rows, OWN * LANES), bf16),
            vmem(operands[1].shape, f32), vmem(operands[0].shape, bf16),
            pltpu.SemaphoreType.DMA((8,)), pltpu.SemaphoreType.DMA((4,)),
            pltpu.SemaphoreType.DMA((4,)), pltpu.SemaphoreType.DMA((4,)),
        ],
        compiler_params=pltpu.CompilerParams(
            collective_id=0, has_side_effects=True, vmem_limit_bytes=VMEM_LIMIT
        ),
    )(*(pltpu.with_memory_space_constraint(x, pltpu.HBM) for x in operands))
    return out_of_pairs(result)


def solution(mesh):
    return jax.shard_map(
        body,
        mesh=mesh,
        in_specs=(P(None, "chan", "seq"), P(None, "chan", None), P("chan", "seq"), P("chan")),
        out_specs=P("chan", "seq"),
        check_vma=False,
    )
```

```python
import functools
import math

import jax
import jax.numpy as jnp
import ml_dtypes
import numpy as np
from jax import lax
from jax.experimental import pallas as pl
from jax.experimental.pallas import tpu as pltpu
from jax.sharding import PartitionSpec as P

LANES = 128
OWN = 2
VMEM_LIMIT = 48 * 1024 * 1024


def halves(table):
    high = table.astype(ml_dtypes.bfloat16)
    low = (table - high.astype(np.float64)).astype(ml_dtypes.bfloat16)
    return np.stack([high, low])


def tables(rows):
    row = np.arange(rows)
    lane = np.arange(LANES)
    angle = (2.0 * math.pi / (4 * rows)) * ((2 * row[:, None] + 1) * row[None, :] % (4 * rows))
    outer = np.concatenate([np.cos(angle), -np.sin(angle)], axis=0)
    outer_back = outer.T / (rows * LANES)
    angle = (2.0 * math.pi / LANES) * (lane[:, None] * lane[None, :] % LANES)
    cos, sin = np.cos(angle), np.sin(angle)
    inner = np.block([[cos, -sin], [sin, cos]])
    angle = (2.0 * math.pi / (4 * rows * LANES)) * ((2 * row[:, None] + 1) * lane[None, :])
    turn = np.stack([np.cos(angle), np.sin(angle)]).astype(np.float32)
    return halves(outer), halves(outer_back), np.concatenate([halves(inner), halves(inner.T)]), turn


def slow_first(peers):
    steps = [(y, z, core) for y in range(max(1, peers // 8)) for z in range(min(4, peers // 2)) for core in range(2)]
    toll = (0, 4.5, 6, 2)
    return sorted(steps[2:], key=lambda step: toll[step[0]] + toll[step[1]] + 2 * (1 - step[2]), reverse=True)


def split(x):
    high = x.astype(jnp.bfloat16)
    return high, (x - high.astype(jnp.float32)).astype(jnp.bfloat16)


def dot(a, b):
    return jnp.dot(a, b, preferred_element_type=jnp.float32)


def left(table, x):
    high, low = split(x)
    return dot(table[0], high) + dot(table[0], low) + dot(table[1], high)


def right(x, high_table, low_table):
    high, low = split(x)
    return dot(high, high_table) + dot(low, high_table) + dot(high, low_table)


def forward(x, rows, outer, inner, turn):
    part = left(outer, x)
    cos, sin = turn[0], turn[1]
    turned = []
    for c in range(OWN):
        re = part[:rows, c * LANES:(c + 1) * LANES]
        im = part[rows:, c * LANES:(c + 1) * LANES]
        turned.append(jnp.concatenate([re * cos + im * sin, im * cos - re * sin], axis=1))
    return right(jnp.concatenate(turned, axis=0), inner[0], inner[1])


def backward(y, rows, outer_back, inner, turn, turned):
    part = right(y, inner[2], inner[3])
    cos, sin = turn[0], turn[1]
    for c in range(OWN):
        lanes = slice(c * LANES, (c + 1) * LANES)
        re = part[c * rows:(c + 1) * rows, :LANES]
        im = part[c * rows:(c + 1) * rows, LANES:]
        turned[0, :rows, lanes], turned[1, :rows, lanes] = split(re * cos - im * sin)
        turned[0, rows:, lanes], turned[1, rows:, lanes] = split(im * cos + re * sin)
    high, low = turned[0], turned[1]
    return dot(outer_back[0], high) + dot(outer_back[0], low) + dot(outer_back[1], high)


def multiply(a, b):
    a_re, a_im, b_re, b_im = a[:, :LANES], a[:, LANES:], b[:, :LANES], b[:, LANES:]
    return jnp.concatenate([a_re * b_re - a_im * b_im, a_re * b_im + a_im * b_re], axis=1)


def short_conv(x, taps, lane, first):
    one = pltpu.roll(x, 1, 1)
    two = pltpu.roll(x, 2, 1)
    one_up = jnp.where(first, 0.0, pltpu.roll(one, 1, 0))
    two_up = jnp.where(first, 0.0, pltpu.roll(two, 1, 0))
    one = jnp.where(lane < 1, one_up, one)
    two = jnp.where(lane < 2, two_up, two)
    return taps[0] * x + taps[1] * one + taps[2] * two


def kernel(
    peers, streams_hbm, filter_hbm, taps_hbm, skip_hbm, outer_hbm, back_hbm, inner_hbm, turn_hbm,
    out,
    taps_v, skip_v, outer, back, inner, turn,
    filter_in, pair_in, query_in, wide, gated_out, turned, filt, streams,
    load_sem, own_sem, send_sem, recv_sem,
):
    rows = 8 * peers
    channels = OWN * peers
    me = lax.axis_index("seq")
    y, z = me // 8, me // 2 % 4
    to_y, to_z = (jnp.where(at >= 2, 1, 3) for at in (y, z))
    ring_at = [lax.rem(y + to_y * d, 4) * 8 for d in range(4)]
    column_at = [lax.rem(z + to_z * d, 4) * 2 for d in range(4)]
    order = [ring_at[a] + column_at[b] + core for a, b, core in slow_first(peers)]
    order.append(me + 1 - 2 * (me % 2))

    barrier = pltpu.get_barrier_semaphore()
    for peer in order:
        pl.semaphore_signal(
            barrier, inc=1, device_id={"seq": peer}, device_id_type=pl.DeviceIdType.MESH
        )

    def load(i, source, target):
        copy = pltpu.make_async_copy(source, target, load_sem.at[i])
        copy.start()
        return copy

    own_loads = [load(6, streams_hbm, streams), load(7, filter_hbm, filt)]
    links = (
        (lambda p: filt.at[p // 4, :, p % 4], lambda p: filter_in.at[p]),
        (lambda p: streams.at[pl.ds(1, 2), p // 4, :, p % 4], lambda p: pair_in.at[:, p]),
        (lambda p: streams.at[0, p // 4, :, p % 4], lambda p: query_in.at[p]),
        (lambda p: gated_out.at[p], lambda p: out.at[p // 4, :, p % 4]),
    )

    def start(index, peer):
        source_of, target_of = links[index]
        pltpu.make_async_remote_copy(
            src_ref=source_of(peer),
            dst_ref=target_of(me),
            send_sem=send_sem.at[index],
            recv_sem=recv_sem.at[index],
            device_id={"seq": peer},
            device_id_type=pl.DeviceIdType.MESH,
        ).start()

    def keep(index):
        source_of, target_of = links[index]
        own = pltpu.make_async_copy(source_of(me), target_of(me), own_sem.at[index])
        own.start()
        return own

    def wait(others, sem):
        pltpu.make_async_copy(others, others, sem).wait()

    for copy in own_loads:
        copy.wait()
    owns = [keep(index) for index in range(3)]
    pl.semaphore_wait(barrier, peers - 1)
    for index in (1, 0, 2):
        for peer in order:
            start(index, peer)
    loads = [
        load(0, outer_hbm, outer), load(1, turn_hbm, turn), load(2, inner_hbm, inner),
        load(3, back_hbm, back), load(4, taps_hbm, taps_v), load(5, skip_hbm, skip_v),
    ]

    rest = pl.ds(0, peers - 1)
    for copy in loads:
        copy.wait()

    def one_channel(ref, c):
        return ref[pl.ds(c, rows, stride=OWN), :]

    lane = lax.broadcasted_iota(jnp.int32, (rows, LANES), 1)
    first = lax.broadcasted_iota(jnp.int32, (rows, LANES), 0) < 1
    channel = lax.broadcasted_iota(jnp.int32, (1, channels), 1)

    def pick(v, own):
        return jnp.sum(jnp.where(channel == own, v, 0.0), axis=1, keepdims=True)

    def shorted(ref, s):
        wide[s] = ref.reshape(OWN * rows, LANES)[...].astype(jnp.float32)
        results = []
        for c in range(OWN):
            taps = [pick(taps_v[s, i:i + 1, :], OWN * me + c) for i in range(3)]
            results.append(short_conv(one_channel(wide.at[s], c), taps, lane, first))
        return results

    owns[1].wait()
    wait(pair_in.at[:, rest], recv_sem.at[1])
    key, value = shorted(pair_in.at[0], 1), shorted(pair_in.at[1], 2)
    mixed = [k * v for k, v in zip(key, value)]
    bins = forward(jnp.concatenate(mixed, axis=1), rows, outer, inner, turn)
    owns[0].wait()
    wait(filter_in.at[rest], recv_sem.at[0])
    pairs = filter_in.reshape(OWN * rows, LANES)
    taken = jnp.concatenate([one_channel(pairs, c) for c in range(OWN)], axis=1)
    filter_bins = forward(taken, rows, outer, inner, turn)

    conv = backward(multiply(bins, filter_bins), rows, back, inner, turn, turned)

    owns[2].wait()
    wait(query_in.at[rest], recv_sem.at[2])
    query = shorted(query_in, 0)
    for c in range(OWN):
        gain = pick(skip_v[...], OWN * me + c)
        gated = query[c] * (conv[:, c * LANES:(c + 1) * LANES] + gain * mixed[c])
        wide[3, pl.ds(c, rows, stride=OWN), :] = gated
    gated_out.reshape(OWN * rows, LANES)[...] = wide[3].astype(jnp.bfloat16)
    for peer in (1, 0):
        pl.when(me != peer)(functools.partial(start, 3, peer))
    for peer in order:
        pl.when(peer >= 2)(functools.partial(start, 3, peer))
    own = keep(3)

    wait(filter_in.at[rest], send_sem.at[0])
    wait(pair_in.at[:, rest], send_sem.at[1])
    wait(query_in.at[rest], send_sem.at[2])
    wait(gated_out.at[rest], send_sem.at[3])
    own.wait()
    wait(gated_out.at[rest], recv_sem.at[3])


def in_pairs(x):
    lead, channels = x.shape[:-2], x.shape[-2]
    x = x.reshape(lead + (channels // 8, 8, 8, LANES))
    return jnp.swapaxes(x, -3, -2).reshape(lead + (channels // 8, 8, 4, OWN, LANES))


def out_of_pairs(x):
    groups = x.shape[0]
    x = jnp.swapaxes(x.reshape(groups, 8, 8, LANES), 1, 2)
    return x.reshape(groups * 8, 8 * LANES)


def body(streams, short_taps, long_filter, skip_gain):
    peers = lax.axis_size("seq")
    rows = 8 * peers
    outer, back, inner, turn = (jnp.asarray(t) for t in tables(rows))
    f32, bf16 = jnp.float32, jnp.bfloat16
    vmem = pltpu.VMEM
    taps = jnp.transpose(short_taps, (0, 2, 1))
    skip = skip_gain.reshape(1, -1)
    operands = (in_pairs(streams), in_pairs(long_filter), taps, skip, outer, back, inner, turn)
    anywhere = pl.BlockSpec(memory_space=pl.ANY)
    one = (peers, 8, OWN, LANES)
    result = pl.pallas_call(
        functools.partial(kernel, peers),
        out_shape=vmem((OWN * peers // 8, 8, 4, OWN, LANES), bf16),
        in_specs=[anywhere] * len(operands),
        out_specs=anywhere,
        scratch_shapes=[
            vmem(taps.shape, f32), vmem(skip.shape, f32),
            vmem(outer.shape, bf16), vmem(back.shape, bf16), vmem(inner.shape, bf16), vmem(turn.shape, f32),
            vmem(one, f32), vmem((2,) + one, bf16), vmem(one, bf16),
            vmem((4, OWN * rows, LANES), f32), vmem(one, bf16), vmem((2, 2 * rows, OWN * LANES), bf16),
            vmem(operands[1].shape, f32), vmem(operands[0].shape, bf16),
            pltpu.SemaphoreType.DMA((8,)), pltpu.SemaphoreType.DMA((4,)),
            pltpu.SemaphoreType.DMA((4,)), pltpu.SemaphoreType.DMA((4,)),
        ],
        compiler_params=pltpu.CompilerParams(
            collective_id=0, has_side_effects=True, vmem_limit_bytes=VMEM_LIMIT
        ),
    )(*(pltpu.with_memory_space_constraint(x, pltpu.HBM) for x in operands))
    return out_of_pairs(result)


def solution(mesh):
    return jax.shard_map(
        body,
        mesh=mesh,
        in_specs=(P(None, "chan", "seq"), P(None, "chan", None), P("chan", "seq"), P("chan")),
        out_specs=P("chan", "seq"),
        check_vma=False,
    )
```

```python
import functools
import math

import jax
import jax.numpy as jnp
import ml_dtypes
import numpy as np
from jax import lax
from jax.experimental import pallas as pl
from jax.experimental.pallas import tpu as pltpu
from jax.sharding import PartitionSpec as P

LANES = 128
OWN = 2
VMEM_LIMIT = 48 * 1024 * 1024


def halves(table):
    high = table.astype(ml_dtypes.bfloat16)
    low = (table - high.astype(np.float64)).astype(ml_dtypes.bfloat16)
    return np.stack([high, low])


def tables(rows):
    row = np.arange(rows)
    lane = np.arange(LANES)
    angle = (2.0 * math.pi / (4 * rows)) * ((2 * row[:, None] + 1) * row[None, :] % (4 * rows))
    outer = np.concatenate([np.cos(angle), -np.sin(angle)], axis=0)
    outer_back = outer.T / (rows * LANES)
    angle = (2.0 * math.pi / LANES) * (lane[:, None] * lane[None, :] % LANES)
    cos, sin = np.cos(angle), np.sin(angle)
    inner = np.block([[cos, -sin], [sin, cos]])
    angle = (2.0 * math.pi / (4 * rows * LANES)) * ((2 * row[:, None] + 1) * lane[None, :])
    turn = np.stack([np.cos(angle), np.sin(angle)]).astype(np.float32)
    return halves(outer), halves(outer_back), np.concatenate([halves(inner), halves(inner.T)]), turn


def slow_first(peers):
    steps = [(y, z, core) for y in range(max(1, peers // 8)) for z in range(min(4, peers // 2)) for core in range(2)]
    toll = (0, 4.5, 6, 2)
    return sorted(steps[2:], key=lambda step: toll[step[0]] + toll[step[1]] + 2 * (1 - step[2]), reverse=True)


def split(x):
    high = x.astype(jnp.bfloat16)
    return high, (x - high.astype(jnp.float32)).astype(jnp.bfloat16)


def dot(a, b):
    return jnp.dot(a, b, preferred_element_type=jnp.float32)


def left(table, x):
    high, low = split(x)
    return dot(table[0], high) + dot(table[0], low) + dot(table[1], high)


def right(x, high_table, low_table):
    high, low = split(x)
    return dot(high, high_table) + dot(low, high_table) + dot(high, low_table)


def forward(x, rows, outer, inner, turn):
    part = left(outer, x)
    cos, sin = turn[0], turn[1]
    turned = []
    for c in range(OWN):
        re = part[:rows, c * LANES:(c + 1) * LANES]
        im = part[rows:, c * LANES:(c + 1) * LANES]
        turned.append(jnp.concatenate([re * cos + im * sin, im * cos - re * sin], axis=1))
    return right(jnp.concatenate(turned, axis=0), inner[0], inner[1])


def backward(y, rows, inner, turn, turned):
    part = right(y, inner[2], inner[3])
    cos, sin = turn[0], turn[1]
    for c in range(OWN):
        lanes = slice(c * LANES, (c + 1) * LANES)
        re = part[c * rows:(c + 1) * rows, :LANES]
        im = part[c * rows:(c + 1) * rows, LANES:]
        turned[0, :rows, lanes], turned[1, :rows, lanes] = split(re * cos - im * sin)
        turned[0, rows:, lanes], turned[1, rows:, lanes] = split(im * cos + re * sin)


def last_matrix(outer_back, turned, some):
    high, low = turned[0], turned[1]
    near, far = outer_back[0, :some], outer_back[1, :some]
    return dot(near, high) + dot(near, low) + dot(far, high)


def multiply(a, b):
    a_re, a_im, b_re, b_im = a[:, :LANES], a[:, LANES:], b[:, :LANES], b[:, LANES:]
    return jnp.concatenate([a_re * b_re - a_im * b_im, a_re * b_im + a_im * b_re], axis=1)


def short_conv(x, taps, lane, first):
    one = pltpu.roll(x, 1, 1)
    two = pltpu.roll(x, 2, 1)
    one_up = jnp.where(first, 0.0, pltpu.roll(one, 1, 0))
    two_up = jnp.where(first, 0.0, pltpu.roll(two, 1, 0))
    one = jnp.where(lane < 1, one_up, one)
    two = jnp.where(lane < 2, two_up, two)
    return taps[0] * x + taps[1] * one + taps[2] * two


def kernel(
    peers, streams_hbm, filter_hbm, taps_hbm, skip_hbm, outer_hbm, back_hbm, inner_hbm, turn_hbm,
    out,
    taps_v, skip_v, outer, back, inner, turn,
    filter_in, pair_in, query_in, wide, gated_out, turned, filt, streams,
    load_sem, own_sem, send_sem, recv_sem,
):
    rows = 8 * peers
    channels = OWN * peers
    me = lax.axis_index("seq")
    y, z = me // 8, me // 2 % 4
    to_y, to_z = (jnp.where(at >= 2, 1, 3) for at in (y, z))
    ring_at = [lax.rem(y + to_y * d, 4) * 8 for d in range(4)]
    column_at = [lax.rem(z + to_z * d, 4) * 2 for d in range(4)]
    order = [ring_at[a] + column_at[b] + core for a, b, core in slow_first(peers)]
    order.append(me + 1 - 2 * (me % 2))

    barrier = pltpu.get_barrier_semaphore()
    for peer in order:
        pl.semaphore_signal(
            barrier, inc=1, device_id={"seq": peer}, device_id_type=pl.DeviceIdType.MESH
        )

    def load(i, source, target):
        copy = pltpu.make_async_copy(source, target, load_sem.at[i])
        copy.start()
        return copy

    own_loads = [load(6, streams_hbm, streams), load(7, filter_hbm, filt)]
    links = (
        (lambda p: filt.at[p // 4, :, p % 4], lambda p: filter_in.at[p]),
        (lambda p: streams.at[pl.ds(1, 2), p // 4, :, p % 4], lambda p: pair_in.at[:, p]),
        (lambda p: streams.at[0, p // 4, :, p % 4], lambda p: query_in.at[p]),
        (lambda p: gated_out.at[p], lambda p: out.at[p // 4, :, p % 4]),
    )

    def start(index, peer):
        source_of, target_of = links[index]
        pltpu.make_async_remote_copy(
            src_ref=source_of(peer),
            dst_ref=target_of(me),
            send_sem=send_sem.at[index],
            recv_sem=recv_sem.at[jnp.where(me < 2, 4, 2) if index == 2 else index],
            device_id={"seq": peer},
            device_id_type=pl.DeviceIdType.MESH,
        ).start()

    def keep(index):
        source_of, target_of = links[index]
        own = pltpu.make_async_copy(source_of(me), target_of(me), own_sem.at[index])
        own.start()
        return own

    first_chip = me < 2

    def wait_some(buffer, senders, sem):
        mine = first_chip if senders == 2 else jnp.logical_not(first_chip)
        for this_one, count in ((mine, senders - 1), (jnp.logical_not(mine), senders)):
            pl.when(this_one)(functools.partial(wait, buffer.at[pl.ds(0, count)], sem))

    def wait(others, sem):
        pltpu.make_async_copy(others, others, sem).wait()

    for copy in own_loads:
        copy.wait()
    owns = [keep(index) for index in range(3)]
    pl.semaphore_wait(barrier, peers - 1)
    for index in (1, 0, 2):
        for peer in order:
            start(index, peer)
    loads = [
        load(0, outer_hbm, outer), load(1, turn_hbm, turn), load(2, inner_hbm, inner),
        load(3, back_hbm, back), load(4, taps_hbm, taps_v), load(5, skip_hbm, skip_v),
    ]

    rest = pl.ds(0, peers - 1)
    for copy in loads:
        copy.wait()

    def one_channel(ref, c):
        return ref[pl.ds(c, rows, stride=OWN), :]

    channel = lax.broadcasted_iota(jnp.int32, (1, channels), 1)

    def pick(v, own):
        return jnp.sum(jnp.where(channel == own, v, 0.0), axis=1, keepdims=True)

    taps = [
        [[pick(taps_v[s, i:i + 1, :], OWN * me + c) for i in range(3)] for c in range(OWN)] for s in range(3)
    ]
    gains = [pick(skip_v[...], OWN * me + c) for c in range(OWN)]

    def shorted(ref, s, some):
        lane = lax.broadcasted_iota(jnp.int32, (some, LANES), 1)
        first = lax.broadcasted_iota(jnp.int32, (some, LANES), 0) < 1
        wide[s, :OWN * some] = ref.reshape(OWN * rows, LANES)[:OWN * some].astype(jnp.float32)
        return [
            short_conv(wide[s, pl.ds(c, some, stride=OWN), :], taps[s][c], lane, first) for c in range(OWN)
        ]

    owns[1].wait()
    wait(pair_in.at[:, rest], recv_sem.at[1])
    key, value = shorted(pair_in.at[0], 1, rows), shorted(pair_in.at[1], 2, rows)
    mixed = [k * v for k, v in zip(key, value)]
    bins = forward(jnp.concatenate(mixed, axis=1), rows, outer, inner, turn)
    owns[0].wait()
    wait(filter_in.at[rest], recv_sem.at[0])
    pairs = filter_in.reshape(OWN * rows, LANES)
    taken = jnp.concatenate([one_channel(pairs, c) for c in range(OWN)], axis=1)
    filter_bins = forward(taken, rows, outer, inner, turn)

    backward(multiply(bins, filter_bins), rows, inner, turn, turned)

    def ungated(some):
        conv = last_matrix(back, turned, some)
        return [conv[:, c * LANES:(c + 1) * LANES] + gains[c] * mixed[c][:some] for c in range(OWN)]

    def gate(values, begin, end):
        query = shorted(query_in, 0, end)
        for c in range(OWN):
            wide[3, pl.ds(c, end, stride=OWN), :] = query[c] * values[c]
        cut = pl.ds(OWN * begin, OWN * (end - begin))
        gated_out.reshape(OWN * rows, LANES)[cut] = wide[3, cut].astype(jnp.bfloat16)

    ahead = 16
    values = ungated(ahead)
    owns[2].wait()
    wait_some(query_in, 2, recv_sem.at[4])
    gate(values, 0, ahead)
    for peer in (1, 0):
        pl.when(me != peer)(functools.partial(start, 3, peer))
    wait_some(query_in, peers - 2, recv_sem.at[2])
    all_values = ungated(rows)
    gate(all_values, ahead, rows)
    for peer in order:
        pl.when(peer >= 2)(functools.partial(start, 3, peer))
    own = keep(3)

    wait(filter_in.at[rest], send_sem.at[0])
    wait(pair_in.at[:, rest], send_sem.at[1])
    wait(query_in.at[rest], send_sem.at[2])
    wait(gated_out.at[rest], send_sem.at[3])
    own.wait()
    wait(gated_out.at[rest], recv_sem.at[3])


def in_pairs(x):
    lead, channels = x.shape[:-2], x.shape[-2]
    x = x.reshape(lead + (channels // 8, 8, 8, LANES))
    return jnp.swapaxes(x, -3, -2).reshape(lead + (channels // 8, 8, 4, OWN, LANES))


def out_of_pairs(x):
    groups = x.shape[0]
    x = jnp.swapaxes(x.reshape(groups, 8, 8, LANES), 1, 2)
    return x.reshape(groups * 8, 8 * LANES)


def body(streams, short_taps, long_filter, skip_gain):
    peers = lax.axis_size("seq")
    rows = 8 * peers
    outer, back, inner, turn = (jnp.asarray(t) for t in tables(rows))
    f32, bf16 = jnp.float32, jnp.bfloat16
    vmem = pltpu.VMEM
    taps = jnp.transpose(short_taps, (0, 2, 1))
    skip = skip_gain.reshape(1, -1)
    operands = (in_pairs(streams), in_pairs(long_filter), taps, skip, outer, back, inner, turn)
    anywhere = pl.BlockSpec(memory_space=pl.ANY)
    one = (peers, 8, OWN, LANES)
    result = pl.pallas_call(
        functools.partial(kernel, peers),
        out_shape=vmem((OWN * peers // 8, 8, 4, OWN, LANES), bf16),
        in_specs=[anywhere] * len(operands),
        out_specs=anywhere,
        scratch_shapes=[
            vmem(taps.shape, f32), vmem(skip.shape, f32),
            vmem(outer.shape, bf16), vmem(back.shape, bf16), vmem(inner.shape, bf16), vmem(turn.shape, f32),
            vmem(one, f32), vmem((2,) + one, bf16), vmem(one, bf16),
            vmem((4, OWN * rows, LANES), f32), vmem(one, bf16), vmem((2, 2 * rows, OWN * LANES), bf16),
            vmem(operands[1].shape, f32), vmem(operands[0].shape, bf16),
            pltpu.SemaphoreType.DMA((8,)), pltpu.SemaphoreType.DMA((4,)),
            pltpu.SemaphoreType.DMA((4,)), pltpu.SemaphoreType.DMA((5,)),
        ],
        compiler_params=pltpu.CompilerParams(
            collective_id=0, has_side_effects=True, vmem_limit_bytes=VMEM_LIMIT
        ),
    )(*(pltpu.with_memory_space_constraint(x, pltpu.HBM) for x in operands))
    return out_of_pairs(result)


def solution(mesh):
    return jax.shard_map(
        body,
        mesh=mesh,
        in_specs=(P(None, "chan", "seq"), P(None, "chan", None), P("chan", "seq"), P("chan")),
        out_specs=P("chan", "seq"),
        check_vma=False,
    )
```

```python
import functools
import math

import jax
import jax.numpy as jnp
import ml_dtypes
import numpy as np
from jax import lax
from jax.experimental import pallas as pl
from jax.experimental.pallas import tpu as pltpu
from jax.sharding import PartitionSpec as P

LANES = 128
OWN = 2
VMEM_LIMIT = 48 * 1024 * 1024


def halves(table):
    high = table.astype(ml_dtypes.bfloat16)
    low = (table - high.astype(np.float64)).astype(ml_dtypes.bfloat16)
    return np.stack([high, low])


def tables(rows):
    row = np.arange(rows)
    lane = np.arange(LANES)
    angle = (2.0 * math.pi / (4 * rows)) * ((2 * row[:, None] + 1) * row[None, :] % (4 * rows))
    outer = np.concatenate([np.cos(angle), -np.sin(angle)], axis=0)
    outer_back = outer.T / (rows * LANES)
    angle = (2.0 * math.pi / LANES) * (lane[:, None] * lane[None, :] % LANES)
    cos, sin = np.cos(angle), np.sin(angle)
    inner = np.block([[cos, -sin], [sin, cos]])
    angle = (2.0 * math.pi / (4 * rows * LANES)) * ((2 * row[:, None] + 1) * lane[None, :])
    turn = np.stack([np.cos(angle), np.sin(angle)]).astype(np.float32)
    return halves(outer), halves(outer_back), np.concatenate([halves(inner), halves(inner.T)]), turn


def slow_first(peers):
    steps = [(y, z, core) for y in range(max(1, peers // 8)) for z in range(min(4, peers // 2)) for core in range(2)]
    toll = (0, 3.5, 6, 2.5)
    return sorted(steps[2:], key=lambda step: toll[step[0]] + toll[step[1]] + 3 * (1 - step[2]), reverse=True)


def split(x):
    high = x.astype(jnp.bfloat16)
    return high, (x - high.astype(jnp.float32)).astype(jnp.bfloat16)


def dot(a, b):
    return jnp.dot(a, b, preferred_element_type=jnp.float32)


def left(table, x):
    high, low = split(x)
    return dot(table[0], high) + dot(table[0], low) + dot(table[1], high)


def right(x, high_table, low_table):
    high, low = split(x)
    return dot(high, high_table) + dot(low, high_table) + dot(high, low_table)


def forward(x, rows, outer, inner, turn):
    part = left(outer, x)
    cos, sin = turn[0], turn[1]
    turned = []
    for c in range(OWN):
        re = part[:rows, c * LANES:(c + 1) * LANES]
        im = part[rows:, c * LANES:(c + 1) * LANES]
        turned.append(jnp.concatenate([re * cos + im * sin, im * cos - re * sin], axis=1))
    return right(jnp.concatenate(turned, axis=0), inner[0], inner[1])


def backward(y, rows, inner, turn, turned):
    part = right(y, inner[2], inner[3])
    cos, sin = turn[0], turn[1]
    for c in range(OWN):
        lanes = slice(c * LANES, (c + 1) * LANES)
        re = part[c * rows:(c + 1) * rows, :LANES]
        im = part[c * rows:(c + 1) * rows, LANES:]
        turned[0, :rows, lanes], turned[1, :rows, lanes] = split(re * cos - im * sin)
        turned[0, rows:, lanes], turned[1, rows:, lanes] = split(im * cos + re * sin)


def last_matrix(outer_back, turned, some):
    high, low = turned[0], turned[1]
    near, far = outer_back[0, :some], outer_back[1, :some]
    return dot(near, high) + dot(near, low) + dot(far, high)


def multiply(a, b):
    a_re, a_im, b_re, b_im = a[:, :LANES], a[:, LANES:], b[:, :LANES], b[:, LANES:]
    return jnp.concatenate([a_re * b_re - a_im * b_im, a_re * b_im + a_im * b_re], axis=1)


def short_conv(x, taps, lane, first):
    one = pltpu.roll(x, 1, 1)
    two = pltpu.roll(x, 2, 1)
    one_up = jnp.where(first, 0.0, pltpu.roll(one, 1, 0))
    two_up = jnp.where(first, 0.0, pltpu.roll(two, 1, 0))
    one = jnp.where(lane < 1, one_up, one)
    two = jnp.where(lane < 2, two_up, two)
    return taps[0] * x + taps[1] * one + taps[2] * two


def kernel(
    peers, streams_hbm, filter_hbm, taps_hbm, skip_hbm, outer_hbm, back_hbm, inner_hbm, turn_hbm,
    out,
    taps_v, skip_v, outer, back, inner, turn,
    filter_in, pair_in, query_in, wide, gated_out, turned, filt, streams,
    load_sem, own_sem, send_sem, recv_sem,
):
    rows = 8 * peers
    channels = OWN * peers
    me = lax.axis_index("seq")
    y, z = me // 8, me // 2 % 4
    to_y, to_z = (jnp.where(at >= 2, 1, 3) for at in (y, z))
    ring_at = [lax.rem(y + to_y * d, 4) * 8 for d in range(4)]
    column_at = [lax.rem(z + to_z * d, 4) * 2 for d in range(4)]
    order = [ring_at[a] + column_at[b] + core for a, b, core in slow_first(peers)]
    order.append(me + 1 - 2 * (me % 2))

    barrier = pltpu.get_barrier_semaphore()
    for peer in order:
        pl.semaphore_signal(
            barrier, inc=1, device_id={"seq": peer}, device_id_type=pl.DeviceIdType.MESH
        )

    def load(i, source, target):
        copy = pltpu.make_async_copy(source, target, load_sem.at[i])
        copy.start()
        return copy

    own_loads = [
        load(6, streams_hbm.at[pl.ds(1, 2)], streams.at[pl.ds(1, 2)]),
        load(7, filter_hbm, filt),
        load(8, streams_hbm.at[0], streams.at[0]),
    ]
    links = (
        (lambda p: filt.at[p // 4, :, p % 4], lambda p: filter_in.at[p]),
        (lambda p: streams.at[pl.ds(1, 2), p // 4, :, p % 4], lambda p: pair_in.at[:, p]),
        (lambda p: streams.at[0, p // 4, :, p % 4], lambda p: query_in.at[p]),
        (lambda p: gated_out.at[p], lambda p: out.at[p // 4, :, p % 4]),
    )

    def start(index, peer):
        source_of, target_of = links[index]
        pltpu.make_async_remote_copy(
            src_ref=source_of(peer),
            dst_ref=target_of(me),
            send_sem=send_sem.at[index],
            recv_sem=recv_sem.at[jnp.where(me < 2, 4, 2) if index == 2 else index],
            device_id={"seq": peer},
            device_id_type=pl.DeviceIdType.MESH,
        ).start()

    def keep(index):
        source_of, target_of = links[index]
        own = pltpu.make_async_copy(source_of(me), target_of(me), own_sem.at[index])
        own.start()
        return own

    first_chip = me < 2

    def wait_some(buffer, senders, sem):
        mine = first_chip if senders == 2 else jnp.logical_not(first_chip)
        for this_one, count in ((mine, senders - 1), (jnp.logical_not(mine), senders)):
            pl.when(this_one)(functools.partial(wait, buffer.at[pl.ds(0, count)], sem))

    def wait(others, sem):
        pltpu.make_async_copy(others, others, sem).wait()

    pl.semaphore_wait(barrier, peers - 1)
    for index, own_load in zip((1, 0, 2), own_loads):
        own_load.wait()
        for peer in order:
            start(index, peer)
    owns = [keep(index) for index in range(3)]
    loads = [
        load(0, outer_hbm, outer), load(1, turn_hbm, turn), load(2, inner_hbm, inner),
        load(3, back_hbm, back), load(4, taps_hbm, taps_v), load(5, skip_hbm, skip_v),
    ]

    rest = pl.ds(0, peers - 1)
    for copy in loads:
        copy.wait()

    def one_channel(ref, c):
        return ref[pl.ds(c, rows, stride=OWN), :]

    channel = lax.broadcasted_iota(jnp.int32, (1, channels), 1)

    def pick(v, own):
        return jnp.sum(jnp.where(channel == own, v, 0.0), axis=1, keepdims=True)

    taps = [
        [[pick(taps_v[s, i:i + 1, :], OWN * me + c) for i in range(3)] for c in range(OWN)] for s in range(3)
    ]
    gains = [pick(skip_v[...], OWN * me + c) for c in range(OWN)]

    def shorted(ref, s, some):
        lane = lax.broadcasted_iota(jnp.int32, (some, LANES), 1)
        first = lax.broadcasted_iota(jnp.int32, (some, LANES), 0) < 1
        wide[s, :OWN * some] = ref.reshape(OWN * rows, LANES)[:OWN * some].astype(jnp.float32)
        return [
            short_conv(wide[s, pl.ds(c, some, stride=OWN), :], taps[s][c], lane, first) for c in range(OWN)
        ]

    owns[1].wait()
    wait(pair_in.at[:, rest], recv_sem.at[1])
    key, value = shorted(pair_in.at[0], 1, rows), shorted(pair_in.at[1], 2, rows)
    mixed = [k * v for k, v in zip(key, value)]
    bins = forward(jnp.concatenate(mixed, axis=1), rows, outer, inner, turn)
    owns[0].wait()
    wait(filter_in.at[rest], recv_sem.at[0])
    pairs = filter_in.reshape(OWN * rows, LANES)
    taken = jnp.concatenate([one_channel(pairs, c) for c in range(OWN)], axis=1)
    filter_bins = forward(taken, rows, outer, inner, turn)

    backward(multiply(bins, filter_bins), rows, inner, turn, turned)

    def ungated(some):
        conv = last_matrix(back, turned, some)
        return [conv[:, c * LANES:(c + 1) * LANES] + gains[c] * mixed[c][:some] for c in range(OWN)]

    def gate(values, begin, end):
        query = shorted(query_in, 0, end)
        for c in range(OWN):
            wide[3, pl.ds(c, end, stride=OWN), :] = query[c] * values[c]
        cut = pl.ds(OWN * begin, OWN * (end - begin))
        gated_out.reshape(OWN * rows, LANES)[cut] = wide[3, cut].astype(jnp.bfloat16)

    ahead = 16
    values = ungated(ahead)
    owns[2].wait()
    wait_some(query_in, 2, recv_sem.at[4])
    gate(values, 0, ahead)
    for peer in (1, 0):
        pl.when(me != peer)(functools.partial(start, 3, peer))
    wait_some(query_in, peers - 2, recv_sem.at[2])
    all_values = ungated(rows)
    gate(all_values, ahead, rows)
    for peer in order:
        pl.when(peer >= 2)(functools.partial(start, 3, peer))
    own = keep(3)

    wait(filter_in.at[rest], send_sem.at[0])
    wait(pair_in.at[:, rest], send_sem.at[1])
    wait(query_in.at[rest], send_sem.at[2])
    wait(gated_out.at[rest], send_sem.at[3])
    own.wait()
    wait(gated_out.at[rest], recv_sem.at[3])


def in_pairs(x):
    lead, channels = x.shape[:-2], x.shape[-2]
    x = x.reshape(lead + (channels // 8, 8, 8, LANES))
    return jnp.swapaxes(x, -3, -2).reshape(lead + (channels // 8, 8, 4, OWN, LANES))


def out_of_pairs(x):
    groups = x.shape[0]
    x = jnp.swapaxes(x.reshape(groups, 8, 8, LANES), 1, 2)
    return x.reshape(groups * 8, 8 * LANES)


def body(streams, short_taps, long_filter, skip_gain):
    peers = lax.axis_size("seq")
    rows = 8 * peers
    outer, back, inner, turn = (jnp.asarray(t) for t in tables(rows))
    f32, bf16 = jnp.float32, jnp.bfloat16
    vmem = pltpu.VMEM
    taps = jnp.transpose(short_taps, (0, 2, 1))
    skip = skip_gain.reshape(1, -1)
    operands = (in_pairs(streams), in_pairs(long_filter), taps, skip, outer, back, inner, turn)
    anywhere = pl.BlockSpec(memory_space=pl.ANY)
    one = (peers, 8, OWN, LANES)
    result = pl.pallas_call(
        functools.partial(kernel, peers),
        out_shape=vmem((OWN * peers // 8, 8, 4, OWN, LANES), bf16),
        in_specs=[anywhere] * len(operands),
        out_specs=anywhere,
        scratch_shapes=[
            vmem(taps.shape, f32), vmem(skip.shape, f32),
            vmem(outer.shape, bf16), vmem(back.shape, bf16), vmem(inner.shape, bf16), vmem(turn.shape, f32),
            vmem(one, f32), vmem((2,) + one, bf16), vmem(one, bf16),
            vmem((4, OWN * rows, LANES), f32), vmem(one, bf16), vmem((2, 2 * rows, OWN * LANES), bf16),
            vmem(operands[1].shape, f32), vmem(operands[0].shape, bf16),
            pltpu.SemaphoreType.DMA((9,)), pltpu.SemaphoreType.DMA((4,)),
            pltpu.SemaphoreType.DMA((4,)), pltpu.SemaphoreType.DMA((5,)),
        ],
        compiler_params=pltpu.CompilerParams(
            collective_id=0, has_side_effects=True, vmem_limit_bytes=VMEM_LIMIT
        ),
    )(*(pltpu.with_memory_space_constraint(x, pltpu.HBM) for x in operands))
    return out_of_pairs(result)


def solution(mesh):
    return jax.shard_map(
        body,
        mesh=mesh,
        in_specs=(P(None, "chan", "seq"), P(None, "chan", None), P("chan", "seq"), P("chan")),
        out_specs=P("chan", "seq"),
        check_vma=False,
    )
```

```python
import functools
import math

import jax
import jax.numpy as jnp
import ml_dtypes
import numpy as np
from jax import lax
from jax.experimental import pallas as pl
from jax.experimental.pallas import tpu as pltpu
from jax.sharding import PartitionSpec as P

LANES = 128
OWN = 2
VMEM_LIMIT = 48 * 1024 * 1024


def halves(table):
    high = table.astype(ml_dtypes.bfloat16)
    low = (table - high.astype(np.float64)).astype(ml_dtypes.bfloat16)
    return np.stack([high, low])


def tables(rows):
    row = np.arange(rows)
    lane = np.arange(LANES)
    angle = (2.0 * math.pi / (4 * rows)) * ((2 * row[:, None] + 1) * row[None, :] % (4 * rows))
    outer = np.concatenate([np.cos(angle), -np.sin(angle)], axis=0)
    outer_back = outer.T / (rows * LANES)
    angle = (2.0 * math.pi / LANES) * (lane[:, None] * lane[None, :] % LANES)
    cos, sin = np.cos(angle), np.sin(angle)
    inner = np.block([[cos, -sin], [sin, cos]])
    angle = (2.0 * math.pi / (4 * rows * LANES)) * ((2 * row[:, None] + 1) * lane[None, :])
    turn = np.stack([np.cos(angle), np.sin(angle)]).astype(np.float32)
    return halves(outer), halves(outer_back), np.concatenate([halves(inner), halves(inner.T)]), turn


def slow_first(peers):
    steps = [(y, z, core) for y in range(max(1, peers // 8)) for z in range(min(4, peers // 2)) for core in range(2)]
    toll = (0, 3.5, 6, 2.5)
    return sorted(steps[2:], key=lambda step: toll[step[0]] + toll[step[1]] + 3 * (1 - step[2]), reverse=True)


def split(x):
    high = x.astype(jnp.bfloat16)
    return high, (x - high.astype(jnp.float32)).astype(jnp.bfloat16)


def dot(a, b):
    return jnp.dot(a, b, preferred_element_type=jnp.float32)


def left(table, x):
    high, low = split(x)
    return dot(table[0], high) + dot(table[0], low) + dot(table[1], high)


def right(x, high_table, low_table):
    high, low = split(x)
    return dot(high, high_table) + dot(low, high_table) + dot(high, low_table)


def forward(x, rows, outer, inner, turn):
    part = left(outer, x)
    cos, sin = turn[0], turn[1]
    turned = []
    for c in range(OWN):
        re = part[:rows, c * LANES:(c + 1) * LANES]
        im = part[rows:, c * LANES:(c + 1) * LANES]
        turned.append(jnp.concatenate([re * cos + im * sin, im * cos - re * sin], axis=1))
    return right(jnp.concatenate(turned, axis=0), inner[0], inner[1])


def backward(y, rows, inner, turn, turned):
    part = right(y, inner[2], inner[3])
    cos, sin = turn[0], turn[1]
    for c in range(OWN):
        lanes = slice(c * LANES, (c + 1) * LANES)
        re = part[c * rows:(c + 1) * rows, :LANES]
        im = part[c * rows:(c + 1) * rows, LANES:]
        turned[0, :rows, lanes], turned[1, :rows, lanes] = split(re * cos - im * sin)
        turned[0, rows:, lanes], turned[1, rows:, lanes] = split(im * cos + re * sin)


def last_matrix(outer_back, turned, some):
    high, low = turned[0], turned[1]
    near, far = outer_back[0, :some], outer_back[1, :some]
    both = dot(jnp.concatenate([near, far], axis=0), high)
    return both[:some] + dot(near, low) + both[some:]


def multiply(a, b):
    a_re, a_im, b_re, b_im = a[:, :LANES], a[:, LANES:], b[:, :LANES], b[:, LANES:]
    return jnp.concatenate([a_re * b_re - a_im * b_im, a_re * b_im + a_im * b_re], axis=1)


def short_conv(x, taps, lane, first):
    one = pltpu.roll(x, 1, 1)
    two = pltpu.roll(x, 2, 1)
    one_up = jnp.where(first, 0.0, pltpu.roll(one, 1, 0))
    two_up = jnp.where(first, 0.0, pltpu.roll(two, 1, 0))
    one = jnp.where(lane < 1, one_up, one)
    two = jnp.where(lane < 2, two_up, two)
    return taps[0] * x + taps[1] * one + taps[2] * two


def kernel(
    peers, streams_hbm, filter_hbm, taps_hbm, skip_hbm, outer_hbm, back_hbm, inner_hbm, turn_hbm,
    out,
    taps_v, skip_v, outer, back, inner, turn,
    filter_in, pair_in, query_in, wide, gated_out, turned, filt, streams,
    load_sem, own_sem, send_sem, recv_sem,
):
    rows = 8 * peers
    channels = OWN * peers
    me = lax.axis_index("seq")
    y, z = me // 8, me // 2 % 4
    to_y, to_z = (jnp.where(at >= 2, 1, 3) for at in (y, z))
    ring_at = [lax.rem(y + to_y * d, 4) * 8 for d in range(4)]
    column_at = [lax.rem(z + to_z * d, 4) * 2 for d in range(4)]
    order = [ring_at[a] + column_at[b] + core for a, b, core in slow_first(peers)]
    order.append(me + 1 - 2 * (me % 2))

    barrier = pltpu.get_barrier_semaphore()
    for peer in order:
        pl.semaphore_signal(
            barrier, inc=1, device_id={"seq": peer}, device_id_type=pl.DeviceIdType.MESH
        )

    def load(i, source, target):
        copy = pltpu.make_async_copy(source, target, load_sem.at[i])
        copy.start()
        return copy

    own_loads = [
        load(6, streams_hbm.at[pl.ds(1, 2)], streams.at[pl.ds(1, 2)]),
        load(7, filter_hbm, filt),
        load(8, streams_hbm.at[0], streams.at[0]),
    ]
    links = (
        (lambda p: filt.at[p // 4, :, p % 4], lambda p: filter_in.at[p]),
        (lambda p: streams.at[pl.ds(1, 2), p // 4, :, p % 4], lambda p: pair_in.at[:, p]),
        (lambda p: streams.at[0, p // 4, :, p % 4], lambda p: query_in.at[p]),
        (lambda p: gated_out.at[p], lambda p: out.at[p // 4, :, p % 4]),
    )

    def start(index, peer):
        source_of, target_of = links[index]
        pltpu.make_async_remote_copy(
            src_ref=source_of(peer),
            dst_ref=target_of(me),
            send_sem=send_sem.at[index],
            recv_sem=recv_sem.at[jnp.where(me < 2, 4, 2) if index == 2 else index],
            device_id={"seq": peer},
            device_id_type=pl.DeviceIdType.MESH,
        ).start()

    def keep(index):
        source_of, target_of = links[index]
        own = pltpu.make_async_copy(source_of(me), target_of(me), own_sem.at[index])
        own.start()
        return own

    first_chip = me < 2

    def wait_some(buffer, senders, sem):
        mine = first_chip if senders == 2 else jnp.logical_not(first_chip)
        for this_one, count in ((mine, senders - 1), (jnp.logical_not(mine), senders)):
            pl.when(this_one)(functools.partial(wait, buffer.at[pl.ds(0, count)], sem))

    def wait(others, sem):
        pltpu.make_async_copy(others, others, sem).wait()

    pl.semaphore_wait(barrier, peers - 1)
    own_loads[0].wait()
    for peer in order:
        start(1, peer)
    own_loads[1].wait()
    own_loads[2].wait()
    slow, quick = order[:22], order[22:]
    for peer in slow:
        start(0, peer)
    for peer in slow:
        pl.when(first_chip)(functools.partial(start, 2, peer))
    for peer in quick:
        start(0, peer)
    for peer in slow:
        pl.when(jnp.logical_not(first_chip))(functools.partial(start, 2, peer))
    for peer in quick:
        start(2, peer)
    owns = [keep(index) for index in range(3)]
    loads = [
        load(0, outer_hbm, outer), load(1, turn_hbm, turn), load(2, inner_hbm, inner),
        load(3, back_hbm, back), load(4, taps_hbm, taps_v), load(5, skip_hbm, skip_v),
    ]

    rest = pl.ds(0, peers - 1)
    for copy in loads:
        copy.wait()

    def one_channel(ref, c):
        return ref[pl.ds(c, rows, stride=OWN), :]

    channel = lax.broadcasted_iota(jnp.int32, (1, channels), 1)

    def pick(v, own):
        return jnp.sum(jnp.where(channel == own, v, 0.0), axis=1, keepdims=True)

    taps = [
        [[pick(taps_v[s, i:i + 1, :], OWN * me + c) for i in range(3)] for c in range(OWN)] for s in range(3)
    ]
    gains = [pick(skip_v[...], OWN * me + c) for c in range(OWN)]

    def shorted(ref, s, some):
        lane = lax.broadcasted_iota(jnp.int32, (some, LANES), 1)
        first = lax.broadcasted_iota(jnp.int32, (some, LANES), 0) < 1
        wide[s, :OWN * some] = ref.reshape(OWN * rows, LANES)[:OWN * some].astype(jnp.float32)
        return [
            short_conv(wide[s, pl.ds(c, some, stride=OWN), :], taps[s][c], lane, first) for c in range(OWN)
        ]

    owns[1].wait()
    wait(pair_in.at[:, rest], recv_sem.at[1])
    key, value = shorted(pair_in.at[0], 1, rows), shorted(pair_in.at[1], 2, rows)
    mixed = [k * v for k, v in zip(key, value)]
    bins = forward(jnp.concatenate(mixed, axis=1), rows, outer, inner, turn)
    owns[0].wait()
    wait(filter_in.at[rest], recv_sem.at[0])
    pairs = filter_in.reshape(OWN * rows, LANES)
    taken = jnp.concatenate([one_channel(pairs, c) for c in range(OWN)], axis=1)
    filter_bins = forward(taken, rows, outer, inner, turn)

    backward(multiply(bins, filter_bins), rows, inner, turn, turned)

    def ungated(some):
        conv = last_matrix(back, turned, some)
        return [conv[:, c * LANES:(c + 1) * LANES] + gains[c] * mixed[c][:some] for c in range(OWN)]

    def gate(values, begin, end):
        query = shorted(query_in, 0, end)
        for c in range(OWN):
            wide[3, pl.ds(c, end, stride=OWN), :] = query[c] * values[c]
        cut = pl.ds(OWN * begin, OWN * (end - begin))
        gated_out.reshape(OWN * rows, LANES)[cut] = wide[3, cut].astype(jnp.bfloat16)

    ahead = 16
    values = ungated(ahead)
    owns[2].wait()
    wait_some(query_in, 2, recv_sem.at[4])
    gate(values, 0, ahead)
    for peer in (1, 0):
        pl.when(me != peer)(functools.partial(start, 3, peer))
    wait_some(query_in, peers - 2, recv_sem.at[2])
    all_values = ungated(rows)
    gate(all_values, ahead, rows)
    for peer in order:
        pl.when(peer >= 2)(functools.partial(start, 3, peer))
    own = keep(3)

    wait(filter_in.at[rest], send_sem.at[0])
    wait(pair_in.at[:, rest], send_sem.at[1])
    wait(query_in.at[rest], send_sem.at[2])
    wait(gated_out.at[rest], send_sem.at[3])
    own.wait()
    wait(gated_out.at[rest], recv_sem.at[3])


def in_pairs(x):
    lead, channels = x.shape[:-2], x.shape[-2]
    x = x.reshape(lead + (channels // 8, 8, 8, LANES))
    return jnp.swapaxes(x, -3, -2).reshape(lead + (channels // 8, 8, 4, OWN, LANES))


def out_of_pairs(x):
    groups = x.shape[0]
    x = jnp.swapaxes(x.reshape(groups, 8, 8, LANES), 1, 2)
    return x.reshape(groups * 8, 8 * LANES)


def body(streams, short_taps, long_filter, skip_gain):
    peers = lax.axis_size("seq")
    rows = 8 * peers
    outer, back, inner, turn = (jnp.asarray(t) for t in tables(rows))
    f32, bf16 = jnp.float32, jnp.bfloat16
    vmem = pltpu.VMEM
    taps = jnp.transpose(short_taps, (0, 2, 1))
    skip = skip_gain.reshape(1, -1)
    operands = (in_pairs(streams), in_pairs(long_filter), taps, skip, outer, back, inner, turn)
    anywhere = pl.BlockSpec(memory_space=pl.ANY)
    one = (peers, 8, OWN, LANES)
    result = pl.pallas_call(
        functools.partial(kernel, peers),
        out_shape=vmem((OWN * peers // 8, 8, 4, OWN, LANES), bf16),
        in_specs=[anywhere] * len(operands),
        out_specs=anywhere,
        scratch_shapes=[
            vmem(taps.shape, f32), vmem(skip.shape, f32),
            vmem(outer.shape, bf16), vmem(back.shape, bf16), vmem(inner.shape, bf16), vmem(turn.shape, f32),
            vmem(one, f32), vmem((2,) + one, bf16), vmem(one, bf16),
            vmem((4, OWN * rows, LANES), f32), vmem(one, bf16), vmem((2, 2 * rows, OWN * LANES), bf16),
            vmem(operands[1].shape, f32), vmem(operands[0].shape, bf16),
            pltpu.SemaphoreType.DMA((9,)), pltpu.SemaphoreType.DMA((4,)),
            pltpu.SemaphoreType.DMA((4,)), pltpu.SemaphoreType.DMA((5,)),
        ],
        compiler_params=pltpu.CompilerParams(
            collective_id=0, has_side_effects=True, vmem_limit_bytes=VMEM_LIMIT
        ),
    )(*(pltpu.with_memory_space_constraint(x, pltpu.HBM) for x in operands))
    return out_of_pairs(result)


def solution(mesh):
    return jax.shard_map(
        body,
        mesh=mesh,
        in_specs=(P(None, "chan", "seq"), P(None, "chan", None), P("chan", "seq"), P("chan")),
        out_specs=P("chan", "seq"),
        check_vma=False,
    )
```

```python
import functools
import math

import jax
import jax.numpy as jnp
import ml_dtypes
import numpy as np
from jax import lax
from jax.experimental import pallas as pl
from jax.experimental.pallas import tpu as pltpu
from jax.sharding import PartitionSpec as P

LANES = 128
OWN = 2
VMEM_LIMIT = 48 * 1024 * 1024


def halves(table):
    high = table.astype(ml_dtypes.bfloat16)
    low = (table - high.astype(np.float64)).astype(ml_dtypes.bfloat16)
    return np.stack([high, low])


def tables(rows):
    row = np.arange(rows)
    lane = np.arange(LANES)
    angle = (2.0 * math.pi / (4 * rows)) * ((2 * row[:, None] + 1) * row[None, :] % (4 * rows))
    outer = np.concatenate([np.cos(angle), -np.sin(angle)], axis=0)
    outer_back = outer.T / (rows * LANES)
    angle = (2.0 * math.pi / LANES) * (lane[:, None] * lane[None, :] % LANES)
    cos, sin = np.cos(angle), np.sin(angle)
    inner = np.block([[cos, -sin], [sin, cos]])
    angle = (2.0 * math.pi / (4 * rows * LANES)) * ((2 * row[:, None] + 1) * lane[None, :])
    turn = np.stack([np.cos(angle), np.sin(angle)]).astype(np.float32)
    return halves(outer), halves(outer_back), np.concatenate([halves(inner), halves(inner.T)]), turn


def slow_first(peers):
    steps = [(y, z, core) for y in range(max(1, peers // 8)) for z in range(min(4, peers // 2)) for core in range(2)]
    toll = (0, 3.5, 6, 2.5)
    return sorted(steps[2:], key=lambda step: toll[step[0]] + toll[step[1]] + 3 * (1 - step[2]), reverse=True)


def split(x):
    high = x.astype(jnp.bfloat16)
    return high, (x - high.astype(jnp.float32)).astype(jnp.bfloat16)


def dot(a, b):
    return jnp.dot(a, b, preferred_element_type=jnp.float32)


def left(table, x):
    high, low = split(x)
    return dot(table[0], high) + dot(table[0], low) + dot(table[1], high)


def right(x, high_table, low_table):
    high, low = split(x)
    return dot(high, high_table) + dot(low, high_table) + dot(high, low_table)


def forward(x, rows, outer, inner, turn):
    part = left(outer, x)
    cos, sin = turn[0], turn[1]
    turned = []
    for c in range(OWN):
        re = part[:rows, c * LANES:(c + 1) * LANES]
        im = part[rows:, c * LANES:(c + 1) * LANES]
        turned.append(jnp.concatenate([re * cos + im * sin, im * cos - re * sin], axis=1))
    return right(jnp.concatenate(turned, axis=0), inner[0], inner[1])


def backward(y, rows, inner, turn, turned):
    part = right(y, inner[2], inner[3])
    cos, sin = turn[0], turn[1]
    for c in range(OWN):
        lanes = slice(c * LANES, (c + 1) * LANES)
        re = part[c * rows:(c + 1) * rows, :LANES]
        im = part[c * rows:(c + 1) * rows, LANES:]
        turned[0, :rows, lanes], turned[1, :rows, lanes] = split(re * cos - im * sin)
        turned[0, rows:, lanes], turned[1, rows:, lanes] = split(im * cos + re * sin)


def last_matrix(outer_back, turned, some):
    high, low = turned[0], turned[1]
    near, far = outer_back[0, :some], outer_back[1, :some]
    both = dot(jnp.concatenate([near, far], axis=0), high)
    return both[:some] + dot(near, low) + both[some:]


def multiply(a, b):
    a_re, a_im, b_re, b_im = a[:, :LANES], a[:, LANES:], b[:, :LANES], b[:, LANES:]
    return jnp.concatenate([a_re * b_re - a_im * b_im, a_re * b_im + a_im * b_re], axis=1)


def short_conv(x, taps, lane, first):
    one = pltpu.roll(x, 1, 1)
    two = pltpu.roll(x, 2, 1)
    one_up = jnp.where(first, 0.0, pltpu.roll(one, 1, 0))
    two_up = jnp.where(first, 0.0, pltpu.roll(two, 1, 0))
    one = jnp.where(lane < 1, one_up, one)
    two = jnp.where(lane < 2, two_up, two)
    return taps[0] * x + taps[1] * one + taps[2] * two


def kernel(
    peers, streams_hbm, filter_hbm, taps_hbm, skip_hbm, outer_hbm, back_hbm, inner_hbm, turn_hbm,
    out,
    taps_v, skip_v, outer, back, inner, turn,
    filter_in, pair_in, query_in, wide, gated_out, turned, filt, streams,
    load_sem, own_sem, send_sem, recv_sem,
):
    rows = 8 * peers
    channels = OWN * peers
    me = lax.axis_index("seq")
    y, z = me // 8, me // 2 % 4
    to_y, to_z = (jnp.where(at >= 2, 1, 3) for at in (y, z))
    ring_at = [lax.rem(y + to_y * d, 4) * 8 for d in range(4)]
    column_at = [lax.rem(z + to_z * d, 4) * 2 for d in range(4)]
    order = [ring_at[a] + column_at[b] + core for a, b, core in slow_first(peers)]
    order.append(me + 1 - 2 * (me % 2))

    barrier = pltpu.get_barrier_semaphore()
    def load(i, source, target):
        copy = pltpu.make_async_copy(source, target, load_sem.at[i])
        copy.start()
        return copy

    own_loads = [
        load(6, streams_hbm.at[pl.ds(1, 2)], streams.at[pl.ds(1, 2)]),
        load(7, filter_hbm, filt),
        load(8, streams_hbm.at[0], streams.at[0]),
    ]

    for peer in order:
        pl.semaphore_signal(
            barrier, inc=1, device_id={"seq": peer}, device_id_type=pl.DeviceIdType.MESH
        )

    links = (
        (lambda p: filt.at[p // 4, :, p % 4], lambda p: filter_in.at[p]),
        (lambda p: streams.at[pl.ds(1, 2), p // 4, :, p % 4], lambda p: pair_in.at[:, p]),
        (lambda p: streams.at[0, p // 4, :, p % 4], lambda p: query_in.at[p]),
        (lambda p: gated_out.at[p], lambda p: out.at[p // 4, :, p % 4]),
    )

    def start(index, peer):
        source_of, target_of = links[index]
        pltpu.make_async_remote_copy(
            src_ref=source_of(peer),
            dst_ref=target_of(me),
            send_sem=send_sem.at[index],
            recv_sem=recv_sem.at[jnp.where(me < 2, 4, 2) if index == 2 else index],
            device_id={"seq": peer},
            device_id_type=pl.DeviceIdType.MESH,
        ).start()

    def keep(index):
        source_of, target_of = links[index]
        own = pltpu.make_async_copy(source_of(me), target_of(me), own_sem.at[index])
        own.start()
        return own

    first_chip = me < 2

    def wait_some(buffer, senders, sem):
        mine = first_chip if senders == 2 else jnp.logical_not(first_chip)
        for this_one, count in ((mine, senders - 1), (jnp.logical_not(mine), senders)):
            pl.when(this_one)(functools.partial(wait, buffer.at[pl.ds(0, count)], sem))

    def wait(others, sem):
        pltpu.make_async_copy(others, others, sem).wait()

    pl.semaphore_wait(barrier, peers - 1)
    own_loads[0].wait()
    for peer in order:
        start(1, peer)
    own_loads[1].wait()
    own_loads[2].wait()
    slow, quick = order[:22], order[22:]
    for peer in slow:
        start(0, peer)
    for peer in slow:
        pl.when(first_chip)(functools.partial(start, 2, peer))
    for peer in quick:
        start(0, peer)
    for peer in slow:
        pl.when(jnp.logical_not(first_chip))(functools.partial(start, 2, peer))
    for peer in quick:
        start(2, peer)
    owns = [keep(index) for index in range(3)]
    loads = [
        load(0, outer_hbm, outer), load(1, turn_hbm, turn), load(2, inner_hbm, inner),
        load(3, back_hbm, back), load(4, taps_hbm, taps_v), load(5, skip_hbm, skip_v),
    ]

    rest = pl.ds(0, peers - 1)
    for copy in loads:
        copy.wait()

    def one_channel(ref, c):
        return ref[pl.ds(c, rows, stride=OWN), :]

    channel = lax.broadcasted_iota(jnp.int32, (1, channels), 1)

    def pick(v, own):
        return jnp.sum(jnp.where(channel == own, v, 0.0), axis=1, keepdims=True)

    taps = [
        [[pick(taps_v[s, i:i + 1, :], OWN * me + c) for i in range(3)] for c in range(OWN)] for s in range(3)
    ]
    gains = [pick(skip_v[...], OWN * me + c) for c in range(OWN)]

    def shorted(ref, s, some):
        lane = lax.broadcasted_iota(jnp.int32, (some, LANES), 1)
        first = lax.broadcasted_iota(jnp.int32, (some, LANES), 0) < 1
        wide[s, :OWN * some] = ref.reshape(OWN * rows, LANES)[:OWN * some].astype(jnp.float32)
        return [
            short_conv(wide[s, pl.ds(c, some, stride=OWN), :], taps[s][c], lane, first) for c in range(OWN)
        ]

    owns[1].wait()
    wait(pair_in.at[:, rest], recv_sem.at[1])
    key, value = shorted(pair_in.at[0], 1, rows), shorted(pair_in.at[1], 2, rows)
    mixed = [k * v for k, v in zip(key, value)]
    bins = forward(jnp.concatenate(mixed, axis=1), rows, outer, inner, turn)
    owns[0].wait()
    wait(filter_in.at[rest], recv_sem.at[0])
    pairs = filter_in.reshape(OWN * rows, LANES)
    taken = jnp.concatenate([one_channel(pairs, c) for c in range(OWN)], axis=1)
    filter_bins = forward(taken, rows, outer, inner, turn)

    backward(multiply(bins, filter_bins), rows, inner, turn, turned)

    def ungated(some):
        conv = last_matrix(back, turned, some)
        return [conv[:, c * LANES:(c + 1) * LANES] + gains[c] * mixed[c][:some] for c in range(OWN)]

    def gate(values, begin, end):
        query = shorted(query_in, 0, end)
        for c in range(OWN):
            wide[3, pl.ds(c, end, stride=OWN), :] = query[c] * values[c]
        cut = pl.ds(OWN * begin, OWN * (end - begin))
        gated_out.reshape(OWN * rows, LANES)[cut] = wide[3, cut].astype(jnp.bfloat16)

    ahead = 16
    values = ungated(ahead)
    owns[2].wait()
    wait_some(query_in, 2, recv_sem.at[4])
    gate(values, 0, ahead)
    for peer in (1, 0):
        pl.when(me != peer)(functools.partial(start, 3, peer))
    wait_some(query_in, peers - 2, recv_sem.at[2])
    all_values = ungated(rows)
    gate(all_values, ahead, rows)
    for peer in order:
        pl.when(peer >= 2)(functools.partial(start, 3, peer))
    own = keep(3)

    wait(filter_in.at[rest], send_sem.at[0])
    wait(pair_in.at[:, rest], send_sem.at[1])
    wait(query_in.at[rest], send_sem.at[2])
    wait(gated_out.at[rest], send_sem.at[3])
    own.wait()
    wait(gated_out.at[rest], recv_sem.at[3])


def in_pairs(x):
    lead, channels = x.shape[:-2], x.shape[-2]
    x = x.reshape(lead + (channels // 8, 8, 8, LANES))
    return jnp.swapaxes(x, -3, -2).reshape(lead + (channels // 8, 8, 4, OWN, LANES))


def out_of_pairs(x):
    groups = x.shape[0]
    x = jnp.swapaxes(x.reshape(groups, 8, 8, LANES), 1, 2)
    return x.reshape(groups * 8, 8 * LANES)


def body(streams, short_taps, long_filter, skip_gain):
    peers = lax.axis_size("seq")
    rows = 8 * peers
    outer, back, inner, turn = (jnp.asarray(t) for t in tables(rows))
    f32, bf16 = jnp.float32, jnp.bfloat16
    vmem = pltpu.VMEM
    taps = jnp.transpose(short_taps, (0, 2, 1))
    skip = skip_gain.reshape(1, -1)
    operands = (in_pairs(streams), in_pairs(long_filter), taps, skip, outer, back, inner, turn)
    anywhere = pl.BlockSpec(memory_space=pl.ANY)
    one = (peers, 8, OWN, LANES)
    result = pl.pallas_call(
        functools.partial(kernel, peers),
        out_shape=vmem((OWN * peers // 8, 8, 4, OWN, LANES), bf16),
        in_specs=[anywhere] * len(operands),
        out_specs=anywhere,
        scratch_shapes=[
            vmem(taps.shape, f32), vmem(skip.shape, f32),
            vmem(outer.shape, bf16), vmem(back.shape, bf16), vmem(inner.shape, bf16), vmem(turn.shape, f32),
            vmem(one, f32), vmem((2,) + one, bf16), vmem(one, bf16),
            vmem((4, OWN * rows, LANES), f32), vmem(one, bf16), vmem((2, 2 * rows, OWN * LANES), bf16),
            vmem(operands[1].shape, f32), vmem(operands[0].shape, bf16),
            pltpu.SemaphoreType.DMA((9,)), pltpu.SemaphoreType.DMA((4,)),
            pltpu.SemaphoreType.DMA((4,)), pltpu.SemaphoreType.DMA((5,)),
        ],
        compiler_params=pltpu.CompilerParams(
            collective_id=0, has_side_effects=True, vmem_limit_bytes=VMEM_LIMIT
        ),
    )(*(pltpu.with_memory_space_constraint(x, pltpu.HBM) for x in operands))
    return out_of_pairs(result)


def solution(mesh):
    return jax.shard_map(
        body,
        mesh=mesh,
        in_specs=(P(None, "chan", "seq"), P(None, "chan", None), P("chan", "seq"), P("chan")),
        out_specs=P("chan", "seq"),
        check_vma=False,
    )
```

```python
import functools
import math

import jax
import jax.numpy as jnp
import ml_dtypes
import numpy as np
from jax import lax
from jax.experimental import pallas as pl
from jax.experimental.pallas import tpu as pltpu
from jax.sharding import PartitionSpec as P

LANES = 128
OWN = 2
VMEM_LIMIT = 48 * 1024 * 1024


def halves(table):
    high = table.astype(ml_dtypes.bfloat16)
    low = (table - high.astype(np.float64)).astype(ml_dtypes.bfloat16)
    return np.stack([high, low])


def tables(rows):
    row = np.arange(rows)
    lane = np.arange(LANES)
    angle = (2.0 * math.pi / (4 * rows)) * ((2 * row[:, None] + 1) * row[None, :] % (4 * rows))
    outer = np.concatenate([np.cos(angle), -np.sin(angle)], axis=0)
    outer_back = outer.T / (rows * LANES)
    angle = (2.0 * math.pi / LANES) * (lane[:, None] * lane[None, :] % LANES)
    cos, sin = np.cos(angle), np.sin(angle)
    inner = np.block([[cos, -sin], [sin, cos]])
    angle = (2.0 * math.pi / (4 * rows * LANES)) * ((2 * row[:, None] + 1) * lane[None, :])
    turn = np.stack([np.cos(angle), np.sin(angle)]).astype(np.float32)
    return halves(outer), halves(outer_back), np.concatenate([halves(inner), halves(inner.T)]), turn


def slow_first(peers):
    steps = [(y, z, core) for y in range(max(1, peers // 8)) for z in range(min(4, peers // 2)) for core in range(2)]
    toll = (0, 3.5, 6, 2.5)
    return sorted(steps[2:], key=lambda step: toll[step[0]] + toll[step[1]] + 3 * (1 - step[2]), reverse=True)


def split(x):
    high = x.astype(jnp.bfloat16)
    return high, (x - high.astype(jnp.float32)).astype(jnp.bfloat16)


def dot(a, b):
    return jnp.dot(a, b, preferred_element_type=jnp.float32)


def left(table, x):
    high, low = split(x)
    return dot(table[0], high) + dot(table[0], low) + dot(table[1], high)


def right(x, high_table, low_table):
    high, low = split(x)
    return dot(high, high_table) + dot(low, high_table) + dot(high, low_table)


def forward(x, rows, outer, inner, turn):
    part = left(outer, x)
    cos, sin = turn[0], turn[1]
    turned = []
    for c in range(OWN):
        re = part[:rows, c * LANES:(c + 1) * LANES]
        im = part[rows:, c * LANES:(c + 1) * LANES]
        turned.append(jnp.concatenate([re * cos + im * sin, im * cos - re * sin], axis=1))
    return right(jnp.concatenate(turned, axis=0), inner[0], inner[1])


def backward(y, rows, inner, turn, turned):
    part = right(y, inner[2], inner[3])
    cos, sin = turn[0], turn[1]
    for c in range(OWN):
        lanes = slice(c * LANES, (c + 1) * LANES)
        re = part[c * rows:(c + 1) * rows, :LANES]
        im = part[c * rows:(c + 1) * rows, LANES:]
        turned[0, :rows, lanes], turned[1, :rows, lanes] = split(re * cos - im * sin)
        turned[0, rows:, lanes], turned[1, rows:, lanes] = split(im * cos + re * sin)


def last_matrix(outer_back, turned, some):
    high, low = turned[0], turned[1]
    near, far = outer_back[0, :some], outer_back[1, :some]
    both = dot(jnp.concatenate([near, far], axis=0), high)
    return both[:some] + dot(near, low) + both[some:]


def multiply(a, b):
    a_re, a_im, b_re, b_im = a[:, :LANES], a[:, LANES:], b[:, :LANES], b[:, LANES:]
    return jnp.concatenate([a_re * b_re - a_im * b_im, a_re * b_im + a_im * b_re], axis=1)


def short_conv(x, taps, lane, first):
    one = pltpu.roll(x, 1, 1)
    two = pltpu.roll(x, 2, 1)
    one_up = jnp.where(first, 0.0, pltpu.roll(one, 1, 0))
    two_up = jnp.where(first, 0.0, pltpu.roll(two, 1, 0))
    one = jnp.where(lane < 1, one_up, one)
    two = jnp.where(lane < 2, two_up, two)
    return taps[0] * x + taps[1] * one + taps[2] * two


def kernel(
    peers, streams_hbm, filter_hbm, taps_hbm, skip_hbm, outer_hbm, back_hbm, inner_hbm, turn_hbm,
    out,
    taps_v, skip_v, outer, back, inner, turn,
    filter_in, pair_in, query_in, wide, gated_out, turned, filt, streams,
    load_sem, own_sem, send_sem, recv_sem,
):
    rows = 8 * peers
    channels = OWN * peers
    me = lax.axis_index("seq")
    y, z = me // 8, me // 2 % 4
    to_y, to_z = (jnp.where(at >= 2, 1, 3) for at in (y, z))
    ring_at = [lax.rem(y + to_y * d, 4) * 8 for d in range(4)]
    column_at = [lax.rem(z + to_z * d, 4) * 2 for d in range(4)]
    order = [ring_at[a] + column_at[b] + core for a, b, core in slow_first(peers)]
    order.append(me + 1 - 2 * (me % 2))

    barrier = pltpu.get_barrier_semaphore()
    def load(i, source, target):
        copy = pltpu.make_async_copy(source, target, load_sem.at[i])
        copy.start()
        return copy

    own_loads = [
        load(6, streams_hbm.at[pl.ds(1, 2)], streams.at[pl.ds(1, 2)]),
        load(7, filter_hbm, filt),
        load(8, streams_hbm.at[0], streams.at[0]),
    ]

    for peer in order:
        pl.semaphore_signal(
            barrier, inc=1, device_id={"seq": peer}, device_id_type=pl.DeviceIdType.MESH
        )

    links = (
        (lambda p: filt.at[p // 4, :, p % 4], lambda p: filter_in.at[p]),
        (lambda p: streams.at[pl.ds(1, 2), p // 4, :, p % 4], lambda p: pair_in.at[:, p]),
        (lambda p: streams.at[0, p // 4, :, p % 4], lambda p: query_in.at[p]),
        (lambda p: gated_out.at[p], lambda p: out.at[p // 4, :, p % 4]),
    )

    def start(index, peer):
        source_of, target_of = links[index]
        pltpu.make_async_remote_copy(
            src_ref=source_of(peer),
            dst_ref=target_of(me),
            send_sem=send_sem.at[index],
            recv_sem=recv_sem.at[jnp.where(me < 2, 4, 2) if index == 2 else index],
            device_id={"seq": peer},
            device_id_type=pl.DeviceIdType.MESH,
        ).start()

    def keep(index):
        source_of, target_of = links[index]
        own = pltpu.make_async_copy(source_of(me), target_of(me), own_sem.at[index])
        own.start()
        return own

    first_chip = me < 2

    def wait_some(buffer, senders, sem):
        mine = first_chip if senders == 2 else jnp.logical_not(first_chip)
        for this_one, count in ((mine, senders - 1), (jnp.logical_not(mine), senders)):
            pl.when(this_one)(functools.partial(wait, buffer.at[pl.ds(0, count)], sem))

    def wait(others, sem):
        pltpu.make_async_copy(others, others, sem).wait()

    pl.semaphore_wait(barrier, peers - 1)
    own_loads[0].wait()
    for peer in order:
        start(1, peer)
    own_loads[1].wait()
    own_loads[2].wait()
    slow, quick = order[:26], order[26:]
    for peer in slow:
        start(0, peer)
    for peer in slow:
        pl.when(first_chip)(functools.partial(start, 2, peer))
    for peer in quick:
        start(0, peer)
    for peer in slow:
        pl.when(jnp.logical_not(first_chip))(functools.partial(start, 2, peer))
    for peer in quick:
        start(2, peer)
    owns = [keep(index) for index in range(3)]
    loads = [
        load(0, outer_hbm, outer), load(1, turn_hbm, turn), load(2, inner_hbm, inner),
        load(3, back_hbm, back), load(4, taps_hbm, taps_v), load(5, skip_hbm, skip_v),
    ]

    rest = pl.ds(0, peers - 1)
    for copy in loads:
        copy.wait()

    def one_channel(ref, c):
        return ref[pl.ds(c, rows, stride=OWN), :]

    channel = lax.broadcasted_iota(jnp.int32, (1, channels), 1)

    def pick(v, own):
        return jnp.sum(jnp.where(channel == own, v, 0.0), axis=1, keepdims=True)

    taps = [
        [[pick(taps_v[s, i:i + 1, :], OWN * me + c) for i in range(3)] for c in range(OWN)] for s in range(3)
    ]
    gains = [pick(skip_v[...], OWN * me + c) for c in range(OWN)]

    def shorted(ref, s, some):
        lane = lax.broadcasted_iota(jnp.int32, (some, LANES), 1)
        first = lax.broadcasted_iota(jnp.int32, (some, LANES), 0) < 1
        wide[s, :OWN * some] = ref.reshape(OWN * rows, LANES)[:OWN * some].astype(jnp.float32)
        return [
            short_conv(wide[s, pl.ds(c, some, stride=OWN), :], taps[s][c], lane, first) for c in range(OWN)
        ]

    owns[1].wait()
    wait(pair_in.at[:, rest], recv_sem.at[1])
    key, value = shorted(pair_in.at[0], 1, rows), shorted(pair_in.at[1], 2, rows)
    mixed = [k * v for k, v in zip(key, value)]
    bins = forward(jnp.concatenate(mixed, axis=1), rows, outer, inner, turn)
    owns[0].wait()
    wait(filter_in.at[rest], recv_sem.at[0])
    pairs = filter_in.reshape(OWN * rows, LANES)
    taken = jnp.concatenate([one_channel(pairs, c) for c in range(OWN)], axis=1)
    filter_bins = forward(taken, rows, outer, inner, turn)

    backward(multiply(bins, filter_bins), rows, inner, turn, turned)

    def ungated(some):
        conv = last_matrix(back, turned, some)
        return [conv[:, c * LANES:(c + 1) * LANES] + gains[c] * mixed[c][:some] for c in range(OWN)]

    def gate(values, begin, end):
        query = shorted(query_in, 0, end)
        for c in range(OWN):
            wide[3, pl.ds(c, end, stride=OWN), :] = query[c] * values[c]
        cut = pl.ds(OWN * begin, OWN * (end - begin))
        gated_out.reshape(OWN * rows, LANES)[cut] = wide[3, cut].astype(jnp.bfloat16)

    ahead = 16
    values = ungated(ahead)
    owns[2].wait()
    wait_some(query_in, 2, recv_sem.at[4])
    gate(values, 0, ahead)
    for peer in (1, 0):
        pl.when(me != peer)(functools.partial(start, 3, peer))
    wait_some(query_in, peers - 2, recv_sem.at[2])
    all_values = ungated(rows)
    gate(all_values, ahead, rows)
    for peer in order:
        pl.when(peer >= 2)(functools.partial(start, 3, peer))
    own = keep(3)

    wait(filter_in.at[rest], send_sem.at[0])
    wait(pair_in.at[:, rest], send_sem.at[1])
    wait(query_in.at[rest], send_sem.at[2])
    wait(gated_out.at[rest], send_sem.at[3])
    own.wait()
    wait(gated_out.at[rest], recv_sem.at[3])


def in_pairs(x):
    lead, channels = x.shape[:-2], x.shape[-2]
    x = x.reshape(lead + (channels // 8, 8, 8, LANES))
    return jnp.swapaxes(x, -3, -2).reshape(lead + (channels // 8, 8, 4, OWN, LANES))


def out_of_pairs(x):
    groups = x.shape[0]
    x = jnp.swapaxes(x.reshape(groups, 8, 8, LANES), 1, 2)
    return x.reshape(groups * 8, 8 * LANES)


def body(streams, short_taps, long_filter, skip_gain):
    peers = lax.axis_size("seq")
    rows = 8 * peers
    outer, back, inner, turn = (jnp.asarray(t) for t in tables(rows))
    f32, bf16 = jnp.float32, jnp.bfloat16
    vmem = pltpu.VMEM
    taps = jnp.transpose(short_taps, (0, 2, 1))
    skip = skip_gain.reshape(1, -1)
    operands = (in_pairs(streams), in_pairs(long_filter), taps, skip, outer, back, inner, turn)
    anywhere = pl.BlockSpec(memory_space=pl.ANY)
    one = (peers, 8, OWN, LANES)
    result = pl.pallas_call(
        functools.partial(kernel, peers),
        out_shape=vmem((OWN * peers // 8, 8, 4, OWN, LANES), bf16),
        in_specs=[anywhere] * len(operands),
        out_specs=anywhere,
        scratch_shapes=[
            vmem(taps.shape, f32), vmem(skip.shape, f32),
            vmem(outer.shape, bf16), vmem(back.shape, bf16), vmem(inner.shape, bf16), vmem(turn.shape, f32),
            vmem(one, f32), vmem((2,) + one, bf16), vmem(one, bf16),
            vmem((4, OWN * rows, LANES), f32), vmem(one, bf16), vmem((2, 2 * rows, OWN * LANES), bf16),
            vmem(operands[1].shape, f32), vmem(operands[0].shape, bf16),
            pltpu.SemaphoreType.DMA((9,)), pltpu.SemaphoreType.DMA((4,)),
            pltpu.SemaphoreType.DMA((4,)), pltpu.SemaphoreType.DMA((5,)),
        ],
        compiler_params=pltpu.CompilerParams(
            collective_id=0, has_side_effects=True, vmem_limit_bytes=VMEM_LIMIT
        ),
    )(*(pltpu.with_memory_space_constraint(x, pltpu.HBM) for x in operands))
    return out_of_pairs(result)


def solution(mesh):
    return jax.shard_map(
        body,
        mesh=mesh,
        in_specs=(P(None, "chan", "seq"), P(None, "chan", None), P("chan", "seq"), P("chan")),
        out_specs=P("chan", "seq"),
        check_vma=False,
    )
```
